32 devices in a mesh: row: 8 (over y, x, core), col: 4 (over z).
Axes of the slice: x: 2, y: 2, z: 4, core: 2. Of those that a mesh axis runs over, the one named last changes fastest.
Arguments:
- vorticity_coefficients: bfloat16 [3, 512, 512, 512], P(None, 'row', 'col'), may hold values from -6 to 6
Outputs:
- enstrophy: float32 [512, 512, 512], P('row', 'col')
- normals: bfloat16 [3, 512, 512, 512], P(None, 'row', 'col')
The draws below stay inside these ranges and needn't reach their ends.
All inputs are finite; a program needn't handle non-finite values.
Results may differ from the reference program's by a relative error of at most 0.001.
Values sent between devices are 32-bit elements; how exact they have to be, the bound alone decides.
No kernel may reach another device: no remote copies, remote signals or barrier semaphores. Data moves between devices by JAX's collectives and lax.ppermute only.
A program may use at most 256 MiB of HBM per device.

```python
import math
import jax
import jax.numpy as jnp
from jax import lax

N = 512


def levels(rng, dims, cuts, smallest, largest):
    def one(dim, shards_of):
        heights = jax.random.uniform(jax.random.fold_in(jax.random.fold_in(rng, 6), dim), (shards_of,), jnp.float32, smallest / len(cuts), largest / len(cuts))
        return jnp.repeat(jnp.exp(heights), dims[dim] // shards_of).reshape((-1,) + (1,) * (len(dims) - dim - 1))

    factor_of = one(*cuts[0])
    for cut in cuts[1:]:
        factor_of = factor_of * one(*cut)
    return factor_of


def centred(key, extent, width, limit, shards=(), held_as=jnp.bfloat16):
    gain = levels(key, extent, shards, -0.22, 0.18) if shards else 1.0
    array = jax.random.normal(key, extent, jnp.float32) * width * gain
    return jnp.minimum(jnp.maximum(array, -limit), limit).astype(held_as)


def setup_inputs(seed: int = 0) -> dict:
    arg_keys = jax.random.split(jax.random.key(seed), 2)
    vorticity_coefficients = centred(arg_keys[0], (3, N, N, N), 1.0, 6.0, ((1, 8), (2, 4)))
    return dict(vorticity_coefficients=vorticity_coefficients)


EXACT_MULTIPLY = lax.Precision.HIGHEST

def fourier_table(length):
    wave_number = jnp.arange(length, dtype=jnp.int32)[:, None]
    position = jnp.arange(length, dtype=jnp.int32)[None, :]
    nyquist = length // 2
    frequency = jnp.where(wave_number <= nyquist, wave_number, wave_number - nyquist)
    phase_index = (frequency * position % length).astype(jnp.int32)
    angle_value = phase_index.astype(jnp.float32) * (2.0 * math.pi / length)
    edge_mode = (wave_number == 0) | (wave_number == nyquist)
    hermitian_weight = jnp.where(edge_mode, math.sqrt(1.0 / length), math.sqrt(2.0 / length)).astype(jnp.float32)
    return jnp.where(wave_number <= nyquist, jnp.cos(angle_value), jnp.sin(angle_value)) * hermitian_weight

def reference(vorticity_coefficients):
    twiddle_table = fourier_table(N)

    def add_component(running, component):
        widened_input = component.astype(jnp.float32)
        first_axis_transform = jnp.einsum('uma,av->vum', widened_input, twiddle_table, precision=EXACT_MULTIPLY)
        along_second = jnp.einsum('xbq,by->xyq', first_axis_transform, twiddle_table, precision=EXACT_MULTIPLY)
        vort_field = jnp.einsum('xyq,qz->xyz', along_second, twiddle_table, precision=EXACT_MULTIPLY)
        return (running + 0.5 * vort_field * vort_field, None)
    enstrophy, unused = lax.scan(add_component, jnp.zeros((N, N, N), jnp.float32), vorticity_coefficients)
    step_x = 0.5 * (jnp.roll(enstrophy, -1, axis=0) - jnp.roll(enstrophy, 1, axis=0))
    step_y = 0.5 * (jnp.roll(enstrophy, -1, axis=1) - jnp.roll(enstrophy, 1, axis=1))
    step_z = 0.5 * (jnp.roll(enstrophy, -1, axis=2) - jnp.roll(enstrophy, 1, axis=2))
    magnitude = jnp.sqrt(step_x * step_x + step_y * step_y + step_z * step_z)
    inverse = 1.0 / jnp.maximum(magnitude, 1.0)
    normals = jnp.stack([-step_x * inverse, -step_y * inverse, -step_z * inverse], axis=0).astype(jnp.bfloat16)
    return (enstrophy, normals)
```

```python
import functools
import math

import jax
import jax.numpy as jnp
import ml_dtypes
import numpy as np
from jax import lax
from jax.experimental import pallas as pl
from jax.experimental.pallas import tpu as pltpu
from jax.sharding import PartitionSpec as P

EXACT = lax.Precision.HIGHEST
TABLE_PARTS = (0, 1, 2, 0, 1, 0)
VALUE_PARTS = (0, 0, 0, 1, 1, 2)
VMEM_BYTES = 48 * 1024 * 1024
SCALE = 1.0


def fourier_table(length):
    wave_number = np.arange(length)[:, None]
    position = np.arange(length)[None, :]
    nyquist = length // 2
    frequency = np.where(wave_number <= nyquist, wave_number, wave_number - nyquist)
    angle = (frequency * position % length) * (2.0 * math.pi / length)
    edge = (wave_number == 0) | (wave_number == nyquist)
    weight = np.where(edge, math.sqrt(1.0 / length), math.sqrt(2.0 / length))
    table = np.where(wave_number <= nyquist, np.cos(angle), np.sin(angle)) * weight
    return table.astype(np.float32)


def table_parts(table):
    parts = []
    rest = table
    for _ in range(3):
        part = rest.astype(ml_dtypes.bfloat16)
        parts.append(part)
        rest = rest - part.astype(np.float32)
    return parts


def value_parts(value):
    high = value.astype(jnp.bfloat16)
    rest = value - high.astype(jnp.float32)
    middle = rest.astype(jnp.bfloat16)
    low = (rest - middle.astype(jnp.float32)).astype(jnp.bfloat16)
    return high, middle, low


def partner(me, step, count):
    if count & (count - 1) == 0:
        return me ^ step
    return (me + step) % count


def sender(me, step, count):
    if count & (count - 1) == 0:
        return me ^ step
    return (me + count - step) % count


ANY = pl.BlockSpec(memory_space=pl.ANY)


def cost(time):
    return pl.CostEstimate(flops=0, bytes_accessed=int(SCALE * time * 3.0e6), transcendentals=0)


def params():
    return pltpu.CompilerParams(vmem_limit_bytes=VMEM_BYTES)


def first_kernel(table_ref, x_ref, *rest, groups):
    outs = rest[-groups:]
    rows = table_ref.shape[0] // 3
    width = rows // groups
    tile, inner, length = x_ref.shape
    flat = [out.reshape(width * tile, inner) for out in outs]

    @pl.loop(0, tile // 2)
    def _(pair):
        block = x_ref[pl.ds(2 * pair, 2)].reshape(2 * inner, length)
        product = lax.dot_general(
            table_ref[...], block, (((1,), (1,)), ((), ())), preferred_element_type=jnp.float32
        )
        total = product[2 * rows :] + product[rows : 2 * rows] + product[:rows]
        for step in range(groups):
            for j in range(2):
                flat[step][pl.ds(2 * pair + j, width, stride=tile), :] = total[
                    step * width : (step + 1) * width, j * inner : (j + 1) * inner
                ]


def ordered_blocks(array, axis, blocks):
    return jnp.concatenate(
        [lax.dynamic_slice_in_dim(array, block, 1, axis=axis) for block in blocks], axis=axis
    )


def first_transform(spectrum, table, ordered, blocks, first, width, after):
    members, span_b, span_q, length = spectrum.shape
    groups = len(blocks)
    out_shape = (members, width, span_b, span_q)
    if span_q % 128 or span_b % 8:
        chosen = jnp.asarray(table).reshape(length, groups, -1)[:, :, first : first + width]
        chosen = ordered_blocks(chosen, 1, blocks)
        outs = jnp.einsum("cbqk,ksx->scxbq", spectrum.astype(jnp.float32), chosen, precision=EXACT)
        return [outs[step] for step in range(groups)]
    operand = ordered[:, :, first : first + width].reshape(-1, length)
    tile = 8
    return pl.pallas_call(
        functools.partial(first_kernel, groups=groups),
        grid=(members, span_b // tile),
        in_specs=[
            pl.BlockSpec(operand.shape, lambda c, b: (0, 0)),
            pl.BlockSpec((None, tile, span_q, length), lambda c, b: (c, b, 0, 0)),
        ]
        + [ANY] * len(after),
        out_specs=[pl.BlockSpec((None, width, tile, span_q), lambda c, b: (c, 0, b, 0))] * groups,
        out_shape=[jax.ShapeDtypeStruct(out_shape, jnp.float32)] * groups,
        compiler_params=params(),
        cost_estimate=cost(22 + width),
        name="first",
    )(operand, spectrum, *after)


def second_kernel(sources_ref, table_ref, *rest, count):
    ins, out_ref, value_ref = rest[:count], rest[-2], rest[-1]
    width, span_b, span_q = ins[0].shape
    for step in range(count):
        at = pl.multiple_of(sources_ref[step] * span_b, 8)
        for j in range(width):
            value_ref[pl.ds(at, span_b), j * span_q : (j + 1) * span_q] = ins[step][j]
    parts = value_parts(value_ref[...])
    stacked = jnp.concatenate([parts[p] for p in VALUE_PARTS], axis=0)
    product = jnp.dot(table_ref[...], stacked, preferred_element_type=jnp.float32)
    groups, _, span_y, _ = out_ref.shape
    for j in range(width):
        out_ref[:, j] = product[:, j * span_q : (j + 1) * span_q].reshape(groups, span_y, span_q)


def second_transform(pieces, table, stacked, sources, groups, after):
    count = len(pieces)
    members, width, span_b, span_q = pieces[0].shape
    length = count * span_b
    span_y = length // groups
    if span_q % 128 or span_b % 8 or span_y % 8:
        chosen = ordered_blocks(jnp.asarray(table).reshape(count, span_b, length), 0, sources)
        chosen = chosen.reshape(count, span_b, groups, span_y)
        return jnp.einsum("scabq,sbgy->gcayq", jnp.stack(pieces), chosen, precision=EXACT)
    tile = 2 if width % 2 == 0 else 1
    out_shape = (groups, members, width, span_y, span_q)
    return pl.pallas_call(
        functools.partial(second_kernel, count=count),
        grid=(members, width // tile),
        in_specs=[
            pl.BlockSpec(memory_space=pltpu.SMEM),
            pl.BlockSpec(stacked.shape, lambda c, a: (0, 0)),
        ]
        + [pl.BlockSpec((None, tile, span_b, span_q), lambda c, a: (c, a, 0, 0))] * count
        + [ANY] * len(after),
        out_specs=pl.BlockSpec(
            (groups, None, tile, span_y, span_q), lambda c, a: (0, c, a, 0, 0)
        ),
        out_shape=jax.ShapeDtypeStruct(out_shape, jnp.float32),
        scratch_shapes=[pltpu.VMEM((length, tile * span_q), jnp.float32)],
        compiler_params=params(),
        cost_estimate=cost(1 + 2 * width),
        name="second",
    )(jnp.stack(sources).astype(jnp.int32), stacked, *pieces, *after)


def third_kernel(table_ref, in_ref, *rest):
    out_ref, low_ref, high_ref = rest[-3:]
    member = pl.program_id(1)
    groups, width, span_y, span_q = in_ref.shape
    value = jnp.concatenate(
        [in_ref[g].reshape(width * span_y, span_q) for g in range(groups)], axis=1
    )
    parts = value_parts(value)
    stacked = jnp.concatenate([parts[p] for p in VALUE_PARTS], axis=1)
    field = jnp.dot(stacked, table_ref[...], preferred_element_type=jnp.float32)
    level = (0.5 * (field * field)).reshape(out_ref.shape)

    @pl.when(member == 0)
    def _():
        out_ref[...] = level

    @pl.when(member > 0)
    def _():
        out_ref[...] += level

    @pl.when(member == pl.num_programs(1) - 1)
    def _():
        low_ref[...] = out_ref[:, :1]
        high_ref[...] = out_ref[:, span_y - 1 :]


def third_transform(received, table, stacked, after):
    groups, members, width, span_y, span_q = received.shape
    length = groups * span_q
    if span_q % 128 or span_y % 8:
        chosen = jnp.asarray(table).reshape(groups, span_q, length)
        field = jnp.einsum("scayq,sqz->cayz", received, chosen, precision=EXACT)
        level = 0.5 * jnp.sum(field * field, axis=0)
        return level, level[:, :1], level[:, -1:]
    tile = 2 if width % 2 == 0 else 1
    return pl.pallas_call(
        third_kernel,
        grid=(width // tile, members),
        in_specs=[
            pl.BlockSpec(stacked.shape, lambda a, c: (0, 0)),
            pl.BlockSpec((groups, None, tile, span_y, span_q), lambda a, c: (0, c, a, 0, 0)),
        ]
        + [ANY] * len(after),
        out_specs=[
            pl.BlockSpec((tile, span_y, length), lambda a, c: (a, 0, 0)),
            pl.BlockSpec((tile, 1, length), lambda a, c: (a, 0, 0)),
            pl.BlockSpec((tile, 1, length), lambda a, c: (a, 0, 0)),
        ],
        out_shape=[
            jax.ShapeDtypeStruct((width, span_y, length), jnp.float32),
            jax.ShapeDtypeStruct((width, 1, length), jnp.float32),
            jax.ShapeDtypeStruct((width, 1, length), jnp.float32),
        ],
        compiler_params=params(),
        cost_estimate=cost(1 + 2 * width),
        name="third",
    )(stacked, received, *after)


def normal_kernel(centre_ref, before_ref, behind_ref, low_ref, high_ref, *rest):
    level_ref, normal_ref = rest[-2:]
    width, span_y, length = centre_ref.shape
    i = pl.program_id(0)
    centre = centre_ref[i]
    before = jnp.where(i == 0, before_ref[0], centre_ref[jnp.maximum(i - 1, 0)])
    behind = jnp.where(i == width - 1, behind_ref[0], centre_ref[jnp.minimum(i + 1, width - 1)])
    row = lax.broadcasted_iota(jnp.int32, (span_y, length), 0)
    left = jnp.where(row == 0, low_ref[i], pltpu.roll(centre, 1, 0))
    right = jnp.where(row == span_y - 1, high_ref[i], pltpu.roll(centre, span_y - 1, 0))
    step_x = 0.5 * (behind - before)
    step_y = 0.5 * (right - left)
    step_z = 0.5 * (pltpu.roll(centre, length - 1, 1) - pltpu.roll(centre, 1, 1))
    magnitude = jnp.sqrt(step_x * step_x + step_y * step_y + step_z * step_z)
    inverse = -1.0 / jnp.maximum(magnitude, 1.0)
    level_ref[0] = centre
    normal_ref[0, 0] = (step_x * inverse).astype(jnp.bfloat16)
    normal_ref[1, 0] = (step_y * inverse).astype(jnp.bfloat16)
    normal_ref[2, 0] = (step_z * inverse).astype(jnp.bfloat16)


def write_normals(centre, before, behind, low, high, first, whole, held):
    width, span_y, length = centre.shape
    before, before_at = before
    behind, behind_at = behind
    held = () if held is None else held
    return pl.pallas_call(
        normal_kernel,
        grid=(width,),
        in_specs=[
            pl.BlockSpec((width, span_y, length), lambda i: (0, 0, 0)),
            pl.BlockSpec((1, span_y, length), lambda i: (before_at, 0, 0)),
            pl.BlockSpec((1, span_y, length), lambda i: (behind_at, 0, 0)),
            pl.BlockSpec((width, 1, length), lambda i: (0, 0, 0)),
            pl.BlockSpec((width, 1, length), lambda i: (0, 0, 0)),
        ]
        + [ANY] * len(held),
        out_specs=[
            pl.BlockSpec((1, span_y, length), lambda i: (first + i, 0, 0)),
            pl.BlockSpec((3, 1, span_y, length), lambda i: (0, first + i, 0, 0)),
        ],
        out_shape=[
            jax.ShapeDtypeStruct((whole, span_y, length), jnp.float32),
            jax.ShapeDtypeStruct((3, whole, span_y, length), jnp.bfloat16),
        ],
        input_output_aliases={5 + k: k for k in range(len(held))},
        compiler_params=params(),
        cost_estimate=cost(1 + width / 2),
        name="normals",
    )(centre, before, behind, low, high, *held)


def slab_widths(half):
    widths = []
    left = half
    while left:
        width = min(2 ** (1 + len(widths)), 10, left)
        widths.append(width)
        left -= width
    return widths


def ring(axis, up):
    count = lax.axis_size(axis)
    return [(i, (i + 1) % count if up else (i - 1) % count) for i in range(count)]


def body(spectrum):
    length = spectrum.shape[3]
    rows = lax.axis_size("row")
    cols = lax.axis_size("col")
    planes = length // rows
    table = fourier_table(length)
    parts = table_parts(table)
    first_table = np.stack([part.T.reshape(rows, planes, length) for part in parts])
    second_table = jnp.asarray(np.concatenate([parts[p].T for p in TABLE_PARTS], axis=1))
    third_table = jnp.asarray(np.concatenate([parts[p] for p in TABLE_PARTS], axis=0))

    half = planes // 2
    widths = slab_widths(planes - half) + slab_widths(half)[::-1]
    starts = []
    at = half
    for width in widths:
        starts.append(at % planes)
        at += width
    slabs = len(widths)
    split = len(slab_widths(planes - half))

    me = lax.axis_index("row")
    targets = [partner(me, step, rows) for step in range(rows)]
    sources = [sender(me, step, rows) for step in range(rows)]
    pairs = [[(i, partner(i, step, rows)) for i in range(rows)] for step in range(rows)]
    ordered = ordered_blocks(jnp.asarray(first_table), 1, targets)

    def first(slab, after):
        outs = first_transform(spectrum, table, ordered, targets, starts[slab], widths[slab], after)
        return [outs[0]] + [
            lax.ppermute(outs[step], "row", pairs[step]) for step in range(1, rows)
        ]

    levels, lows, highs = {}, {}, {}
    low_halo, high_halo = {}, {}
    halo = {}

    def exchange_rows(chosen):
        low = jnp.concatenate([lows[s] for s in chosen], axis=0)
        high = jnp.concatenate([highs[s] for s in chosen], axis=0)
        from_before = lax.ppermute(high, "col", ring("col", True))
        from_behind = lax.ppermute(low, "col", ring("col", False))
        at = 0
        for s in chosen:
            low_halo[s] = from_before[at : at + widths[s]]
            high_halo[s] = from_behind[at : at + widths[s]]
            at += widths[s]

    def exchange_planes():
        halo["before"] = lax.ppermute(levels[split - 1][-1:], "row", ring("row", True))
        halo["behind"] = lax.ppermute(levels[split][:1], "row", ring("row", False))

    held = None

    def normals(slab):
        nonlocal held
        before = (levels[(slab - 1) % slabs], widths[(slab - 1) % slabs] - 1)
        behind = (levels[(slab + 1) % slabs], 0)
        if slab == split:
            before = (halo["before"], 0)
        if slab == split - 1:
            behind = (halo["behind"], 0)
        held = write_normals(
            levels[slab], before, behind, low_halo[slab], high_halo[slab], starts[slab], planes, held
        )

    def third(slab, after):
        levels[slab], lows[slab], highs[slab] = third_transform(
            arrived.pop(slab), table, third_table, after
        )

    def second(slab, after):
        return second_transform(pieces.pop(slab), table, second_table, sources, cols, after)

    pieces, arrived = {}, {}
    pieces[0] = first(0, ())
    pieces[1] = first(1, (pieces[0][0],))
    for slab in range(slabs):
        if slab >= 2:
            third(slab - 2, ())
        spread = second(slab, (levels[slab - 2],) if slab >= 2 else ())
        arrived[slab] = lax.all_to_all(spread, "col", split_axis=0, concat_axis=0, tiled=True)
        if slab + 2 < slabs:
            pieces[slab + 2] = first(slab + 2, (spread,))
    third(slabs - 2, ())
    third(slabs - 1, ())
    exchange_planes()
    exchange_rows(list(range(0, split)))
    exchange_rows(list(range(split, slabs - 1)))
    exchange_rows([slabs - 1])
    for slab in list(range(1, slabs)) + [0]:
        normals(slab)
    return tuple(held)


def solution(mesh):
    return jax.shard_map(
        body,
        mesh=mesh,
        in_specs=(P(None, "row", "col", None),),
        out_specs=(P("row", "col", None), P(None, "row", "col", None)),
        check_vma=False,
    )
```

```python
import functools
import math

import jax
import jax.numpy as jnp
import ml_dtypes
import numpy as np
from jax import lax
from jax.experimental import pallas as pl
from jax.experimental.pallas import tpu as pltpu
from jax.sharding import PartitionSpec as P

EXACT = lax.Precision.HIGHEST
TABLE_PARTS = (0, 1, 2, 0, 1, 0)
VALUE_PARTS = (0, 0, 0, 1, 1, 2)
VMEM_BYTES = 48 * 1024 * 1024
SCALE = 1.0
RISING = (2, 4, 6, 10)
FALLING = (4, 12, 16)


def fourier_table(length):
    wave_number = np.arange(length)[:, None]
    position = np.arange(length)[None, :]
    nyquist = length // 2
    frequency = np.where(wave_number <= nyquist, wave_number, wave_number - nyquist)
    angle = (frequency * position % length) * (2.0 * math.pi / length)
    edge = (wave_number == 0) | (wave_number == nyquist)
    weight = np.where(edge, math.sqrt(1.0 / length), math.sqrt(2.0 / length))
    table = np.where(wave_number <= nyquist, np.cos(angle), np.sin(angle)) * weight
    return table.astype(np.float32)


def table_parts(table):
    parts = []
    rest = table
    for _ in range(3):
        part = rest.astype(ml_dtypes.bfloat16)
        parts.append(part)
        rest = rest - part.astype(np.float32)
    return parts


def value_parts(value):
    high = value.astype(jnp.bfloat16)
    rest = value - high.astype(jnp.float32)
    middle = rest.astype(jnp.bfloat16)
    low = (rest - middle.astype(jnp.float32)).astype(jnp.bfloat16)
    return high, middle, low


def partner(me, step, count):
    if count & (count - 1) == 0:
        return me ^ step
    return (me + step) % count


def sender(me, step, count):
    if count & (count - 1) == 0:
        return me ^ step
    return (me + count - step) % count


ANY = pl.BlockSpec(memory_space=pl.ANY)


def cost(time):
    return pl.CostEstimate(flops=0, bytes_accessed=int(SCALE * time * 3.0e6), transcendentals=0)


def params():
    return pltpu.CompilerParams(vmem_limit_bytes=VMEM_BYTES)


def first_kernel(table_ref, x_ref, *rest, groups, chunk):
    outs = rest[-groups:]
    rows = table_ref.shape[0] // 3
    width = rows // groups
    tile, inner, length = x_ref.shape
    flat = [out.reshape(width * tile, inner) for out in outs]

    @pl.loop(0, tile // chunk)
    def _(part):
        block = x_ref[pl.ds(chunk * part, chunk)].reshape(chunk * inner, length)
        product = lax.dot_general(
            table_ref[...], block, (((1,), (1,)), ((), ())), preferred_element_type=jnp.float32
        )
        total = product[2 * rows :] + product[rows : 2 * rows] + product[:rows]
        for step in range(groups):
            for j in range(chunk):
                flat[step][pl.ds(chunk * part + j, width, stride=tile), :] = total[
                    step * width : (step + 1) * width, j * inner : (j + 1) * inner
                ]


def ordered_blocks(array, axis, blocks):
    return jnp.concatenate(
        [lax.dynamic_slice_in_dim(array, block, 1, axis=axis) for block in blocks], axis=axis
    )


def first_transform(spectrum, table, ordered, blocks, first, width, after):
    members, span_b, span_q, length = spectrum.shape
    groups = ordered.shape[1]
    if span_q % 128 or span_b % 8:
        chosen = jnp.asarray(table).reshape(length, groups, -1)[:, :, first : first + width]
        chosen = chosen if blocks is None else ordered_blocks(chosen, 1, blocks)
        outs = jnp.einsum("cbqk,ksx->scxbq", spectrum.astype(jnp.float32), chosen, precision=EXACT)
        return outs if blocks is None else [outs[step] for step in range(groups)]
    operand = jnp.asarray(ordered[:, :, first : first + width].reshape(-1, length))
    tile = 16 if span_b % 16 == 0 else 8
    chunk = 8
    while chunk > 2 and operand.shape[0] * chunk * span_q > 2**18:
        chunk //= 2
    if blocks is None:
        outs = 1
        out_specs = pl.BlockSpec((groups, None, width, tile, span_q), lambda c, b: (0, c, 0, b, 0))
        out_shape = jax.ShapeDtypeStruct((groups, members, width, span_b, span_q), jnp.float32)
    else:
        outs = groups
        out_specs = [pl.BlockSpec((None, width, tile, span_q), lambda c, b: (c, 0, b, 0))] * groups
        out_shape = [
            jax.ShapeDtypeStruct((members, width, span_b, span_q), jnp.float32)
        ] * groups
    return pl.pallas_call(
        functools.partial(first_kernel, groups=outs, chunk=chunk),
        grid=(members, span_b // tile),
        in_specs=[
            pl.BlockSpec(operand.shape, lambda c, b: (0, 0)),
            pl.BlockSpec((None, tile, span_q, length), lambda c, b: (c, b, 0, 0)),
        ]
        + [ANY] * len(after),
        out_specs=out_specs,
        out_shape=out_shape,
        compiler_params=params(),
        cost_estimate=cost(12 + width),
        name="first",
    )(operand, spectrum, *after)


def second_kernel(sources_ref, table_ref, *rest, count):
    ins, out_ref, value_ref = rest[:count], rest[-2], rest[-1]
    width, span_b, span_q = ins[0].shape
    for step in range(count):
        at = pl.multiple_of(sources_ref[step] * span_b, 8)
        for j in range(width):
            value_ref[pl.ds(at, span_b), j * span_q : (j + 1) * span_q] = ins[step][j]
    parts = value_parts(value_ref[...])
    stacked = jnp.concatenate([parts[p] for p in VALUE_PARTS], axis=0)
    product = jnp.dot(table_ref[...], stacked, preferred_element_type=jnp.float32)
    groups, _, span_y, _ = out_ref.shape
    for j in range(width):
        out_ref[:, j] = product[:, j * span_q : (j + 1) * span_q].reshape(groups, span_y, span_q)


def second_transform(pieces, table, stacked, sources, groups, after):
    count = len(pieces)
    members, width, span_b, span_q = pieces[0].shape
    length = count * span_b
    span_y = length // groups
    if span_q % 128 or span_b % 8 or span_y % 8:
        chosen = ordered_blocks(jnp.asarray(table).reshape(count, span_b, length), 0, sources)
        chosen = chosen.reshape(count, span_b, groups, span_y)
        pieces = jnp.stack([pieces[step] for step in range(count)])
        return jnp.einsum("scabq,sbgy->gcayq", pieces, chosen, precision=EXACT)
    tile = 2 if width % 2 == 0 else 1
    out_shape = (groups, members, width, span_y, span_q)
    if isinstance(pieces, list):
        in_specs = [pl.BlockSpec((None, tile, span_b, span_q), lambda c, a: (c, a, 0, 0))] * count
    else:
        in_specs = [
            pl.BlockSpec((None, None, tile, span_b, span_q), lambda c, a, s=s: (s, c, a, 0, 0))
            for s in range(count)
        ]
        pieces = [pieces] * count
    return pl.pallas_call(
        functools.partial(second_kernel, count=count),
        grid=(members, width // tile),
        in_specs=[
            pl.BlockSpec(memory_space=pltpu.SMEM),
            pl.BlockSpec(stacked.shape, lambda c, a: (0, 0)),
        ]
        + in_specs
        + [ANY] * len(after),
        out_specs=pl.BlockSpec(
            (groups, None, tile, span_y, span_q), lambda c, a: (0, c, a, 0, 0)
        ),
        out_shape=jax.ShapeDtypeStruct(out_shape, jnp.float32),
        scratch_shapes=[pltpu.VMEM((length, tile * span_q), jnp.float32)],
        compiler_params=params(),
        cost_estimate=cost(1 + 2 * width),
        name="second",
    )(jnp.stack(sources).astype(jnp.int32), stacked, *pieces, *after)


def third_kernel(table_ref, in_ref, *rest):
    out_ref, low_ref, high_ref = rest[-3:]
    member = pl.program_id(1)
    groups, width, span_y, span_q = in_ref.shape
    value = jnp.concatenate(
        [in_ref[g].reshape(width * span_y, span_q) for g in range(groups)], axis=1
    )
    parts = value_parts(value)
    stacked = jnp.concatenate([parts[p] for p in VALUE_PARTS], axis=1)
    field = jnp.dot(stacked, table_ref[...], preferred_element_type=jnp.float32)
    level = (0.5 * (field * field)).reshape(out_ref.shape)

    @pl.when(member == 0)
    def _():
        out_ref[...] = level

    @pl.when(member > 0)
    def _():
        out_ref[...] += level

    @pl.when(member == pl.num_programs(1) - 1)
    def _():
        low_ref[...] = out_ref[:, :1]
        high_ref[...] = out_ref[:, span_y - 1 :]


def third_transform(received, table, stacked, after):
    groups, members, width, span_y, span_q = received.shape
    length = groups * span_q
    if span_q % 128 or span_y % 8:
        chosen = jnp.asarray(table).reshape(groups, span_q, length)
        field = jnp.einsum("scayq,sqz->cayz", received, chosen, precision=EXACT)
        level = 0.5 * jnp.sum(field * field, axis=0)
        return level, level[:, :1], level[:, -1:]
    tile = 2 if width % 2 == 0 else 1
    return pl.pallas_call(
        third_kernel,
        grid=(width // tile, members),
        in_specs=[
            pl.BlockSpec(stacked.shape, lambda a, c: (0, 0)),
            pl.BlockSpec((groups, None, tile, span_y, span_q), lambda a, c: (0, c, a, 0, 0)),
        ]
        + [ANY] * len(after),
        out_specs=[
            pl.BlockSpec((tile, span_y, length), lambda a, c: (a, 0, 0)),
            pl.BlockSpec((tile, 1, length), lambda a, c: (a, 0, 0)),
            pl.BlockSpec((tile, 1, length), lambda a, c: (a, 0, 0)),
        ],
        out_shape=[
            jax.ShapeDtypeStruct((width, span_y, length), jnp.float32),
            jax.ShapeDtypeStruct((width, 1, length), jnp.float32),
            jax.ShapeDtypeStruct((width, 1, length), jnp.float32),
        ],
        compiler_params=params(),
        cost_estimate=cost(1 + 2 * width),
        name="third",
    )(stacked, received, *after)


def normal_kernel(centre_ref, before_ref, behind_ref, low_ref, high_ref, *rest):
    level_ref, normal_ref, token_ref = rest[-3:]
    width, span_y, length = centre_ref.shape
    i = pl.program_id(0)
    centre = centre_ref[i]
    before = jnp.where(i == 0, before_ref[0], centre_ref[jnp.maximum(i - 1, 0)])
    behind = jnp.where(i == width - 1, behind_ref[0], centre_ref[jnp.minimum(i + 1, width - 1)])
    row = lax.broadcasted_iota(jnp.int32, (span_y, length), 0)
    left = jnp.where(row == 0, low_ref[i], pltpu.roll(centre, 1, 0))
    right = jnp.where(row == span_y - 1, high_ref[i], pltpu.roll(centre, span_y - 1, 0))
    step_x = 0.5 * (behind - before)
    step_y = 0.5 * (right - left)
    step_z = 0.5 * (pltpu.roll(centre, length - 1, 1) - pltpu.roll(centre, 1, 1))
    magnitude = jnp.sqrt(step_x * step_x + step_y * step_y + step_z * step_z)
    inverse = -1.0 / jnp.maximum(magnitude, 1.0)
    level_ref[0] = centre
    token_ref[...] = jnp.zeros_like(token_ref)
    normal_ref[0, 0] = (step_x * inverse).astype(jnp.bfloat16)
    normal_ref[1, 0] = (step_y * inverse).astype(jnp.bfloat16)
    normal_ref[2, 0] = (step_z * inverse).astype(jnp.bfloat16)


def write_normals(centre, before, behind, low, high, first, whole, held):
    width, span_y, length = centre.shape
    before, before_at = before
    behind, behind_at = behind
    held = () if held is None else held
    return pl.pallas_call(
        normal_kernel,
        grid=(width,),
        in_specs=[
            pl.BlockSpec((width, span_y, length), lambda i: (0, 0, 0)),
            pl.BlockSpec((1, span_y, length), lambda i: (before_at, 0, 0)),
            pl.BlockSpec((1, span_y, length), lambda i: (behind_at, 0, 0)),
            pl.BlockSpec((width, 1, length), lambda i: (0, 0, 0)),
            pl.BlockSpec((width, 1, length), lambda i: (0, 0, 0)),
        ]
        + [ANY] * len(held),
        out_specs=[
            pl.BlockSpec((1, span_y, length), lambda i: (first + i, 0, 0)),
            pl.BlockSpec((3, 1, span_y, length), lambda i: (0, first + i, 0, 0)),
            pl.BlockSpec((8, 128), lambda i: (0, 0)),
        ],
        out_shape=[
            jax.ShapeDtypeStruct((whole, span_y, length), jnp.float32),
            jax.ShapeDtypeStruct((3, whole, span_y, length), jnp.bfloat16),
            jax.ShapeDtypeStruct((8, 128), jnp.float32),
        ],
        input_output_aliases={5 + k: k for k in range(len(held))},
        compiler_params=params(),
        cost_estimate=cost(1 + width / 2),
        name="normals",
    )(centre, before, behind, low, high, *held)


def slab_widths(left, pattern):
    widths = []
    while left:
        width = min(pattern[min(len(widths), len(pattern) - 1)], left)
        widths.append(width)
        left -= width
    return widths


def ring(axis, up):
    count = lax.axis_size(axis)
    return [(i, (i + 1) % count if up else (i - 1) % count) for i in range(count)]


def body(spectrum):
    length = spectrum.shape[3]
    rows = lax.axis_size("row")
    cols = lax.axis_size("col")
    planes = length // rows
    table = fourier_table(length)
    parts = table_parts(table)
    first_table = np.stack([part.T.reshape(rows, planes, length) for part in parts])
    second_table = jnp.asarray(np.concatenate([parts[p].T for p in TABLE_PARTS], axis=1))
    third_table = jnp.asarray(np.concatenate([parts[p] for p in TABLE_PARTS], axis=0))

    half = planes // 2
    rising = slab_widths(planes - half, RISING)
    widths = rising + slab_widths(half, FALLING)[::-1]
    starts = []
    at = half
    for width in widths:
        starts.append(at % planes)
        at += width
    slabs = len(widths)
    split = len(rising)

    me = lax.axis_index("row")
    targets = [partner(me, step, rows) for step in range(rows)]
    sources = [sender(me, step, rows) for step in range(rows)]
    pairs = [[(i, partner(i, step, rows)) for i in range(rows)] for step in range(rows)]
    ordered = ordered_blocks(jnp.asarray(first_table), 1, targets)

    def first(slab, after):
        outs = first_transform(spectrum, table, ordered, targets, starts[slab], widths[slab], after)
        return [outs[0]] + [
            lax.ppermute(outs[step], "row", pairs[step]) for step in range(1, rows)
        ]

    levels, lows, highs = {}, {}, {}
    low_halo, high_halo = {}, {}
    halo = {}

    def exchange_rows(chosen):
        low = jnp.concatenate([lows[s] for s in chosen], axis=0)
        high = jnp.concatenate([highs[s] for s in chosen], axis=0)
        from_before = lax.ppermute(high, "col", ring("col", True))
        from_behind = lax.ppermute(low, "col", ring("col", False))
        at = 0
        for s in chosen:
            low_halo[s] = from_before[at : at + widths[s]]
            high_halo[s] = from_behind[at : at + widths[s]]
            at += widths[s]

    def exchange_planes():
        halo["before"] = lax.ppermute(levels[split - 1][-1:], "row", ring("row", True))
        halo["behind"] = lax.ppermute(levels[split][:1], "row", ring("row", False))

    held = None

    def normals(slab):
        nonlocal held
        before = (levels[(slab - 1) % slabs], widths[(slab - 1) % slabs] - 1)
        behind = (levels[(slab + 1) % slabs], 0)
        if slab == split:
            before = (halo["before"], 0)
        if slab == split - 1:
            behind = (halo["behind"], 0)
        *held, token = write_normals(
            levels[slab], before, behind, low_halo[slab], high_halo[slab], starts[slab], planes, held
        )
        return token

    def third(slab, after):
        levels[slab], lows[slab], highs[slab] = third_transform(
            arrived.pop(slab), table, third_table, after
        )

    def second(slab, after):
        from_whom = sources if slab else [jnp.int32(step) for step in range(rows)]
        return second_transform(pieces[slab], table, second_table, from_whom, cols, after)

    pieces, arrived = {}, {}
    spectral = first_transform(spectrum, table, first_table, None, starts[0], widths[0], ())
    pieces[0] = lax.all_to_all(spectral, "row", split_axis=0, concat_axis=0, tiled=True)
    pieces[1] = first(1, (spectral,))
    for slab in range(slabs):
        after = []
        if slab >= 2:
            after.append(levels[slab - 2])
        if slab + 1 < slabs:
            after.append(pieces[slab + 1][0])
        early = split - 1 <= slabs - 3
        if slab == slabs - 1 and early:
            exchange_rows(list(range(split)))
            for done in range(1, split - 1):
                after.append(normals(done))
        spread = second(slab, after)
        arrived[slab] = lax.all_to_all(spread, "col", split_axis=0, concat_axis=0, tiled=True)
        if slab + 2 < slabs:
            pieces[slab + 2] = first(slab + 2, (pieces[slab + 1][rows - 1],))
        if slab >= 1:
            third(slab - 1, (pieces[slab + 2][0],) if slab + 2 < slabs else (spread,))
    exchange_planes()
    if not early:
        exchange_rows(list(range(split)))
    exchange_rows(list(range(split, slabs - 1)))
    after = [
        normals(done)
        for done in range(split - 1 if early else 1, slabs - 2)
    ]
    third(slabs - 1, after)
    exchange_rows([slabs - 1])
    for slab in list(range(slabs - 2, slabs)) + [0]:
        normals(slab)
    return tuple(held)


def solution(mesh):
    return jax.shard_map(
        body,
        mesh=mesh,
        in_specs=(P(None, "row", "col", None),),
        out_specs=(P("row", "col", None), P(None, "row", "col", None)),
        check_vma=False,
    )
```

```python
import functools
import math

import jax
import jax.numpy as jnp
import ml_dtypes
import numpy as np
from jax import lax
from jax.experimental import pallas as pl
from jax.experimental.pallas import tpu as pltpu
from jax.sharding import PartitionSpec as P

EXACT = lax.Precision.HIGHEST
TABLE_PARTS = (0, 1, 2, 0, 1, 0)
VALUE_PARTS = (0, 0, 0, 1, 1, 2)
VMEM_BYTES = 48 * 1024 * 1024
SCALE = 1.0
PATTERN = (2, 4, 6, 10, 10, 16, 12)
LAST = 4


def fourier_table(length):
    wave_number = np.arange(length)[:, None]
    position = np.arange(length)[None, :]
    nyquist = length // 2
    frequency = np.where(wave_number <= nyquist, wave_number, wave_number - nyquist)
    angle = (frequency * position % length) * (2.0 * math.pi / length)
    edge = (wave_number == 0) | (wave_number == nyquist)
    weight = np.where(edge, math.sqrt(1.0 / length), math.sqrt(2.0 / length))
    table = np.where(wave_number <= nyquist, np.cos(angle), np.sin(angle)) * weight
    return table.astype(np.float32)


def table_parts(table):
    parts = []
    rest = table
    for _ in range(3):
        part = rest.astype(ml_dtypes.bfloat16)
        parts.append(part)
        rest = rest - part.astype(np.float32)
    return parts


def value_parts(value):
    high = value.astype(jnp.bfloat16)
    rest = value - high.astype(jnp.float32)
    middle = rest.astype(jnp.bfloat16)
    low = (rest - middle.astype(jnp.float32)).astype(jnp.bfloat16)
    return high, middle, low


def partner(me, step, count):
    if count & (count - 1) == 0:
        return me ^ step
    return (me + step) % count


def sender(me, step, count):
    if count & (count - 1) == 0:
        return me ^ step
    return (me + count - step) % count


ANY = pl.BlockSpec(memory_space=pl.ANY)


def cost(time):
    return pl.CostEstimate(flops=0, bytes_accessed=int(SCALE * time * 3.0e6), transcendentals=0)


def params():
    return pltpu.CompilerParams(vmem_limit_bytes=VMEM_BYTES)


def first_kernel(table_ref, x_ref, *rest, widths, chunk):
    outs = rest[-len(widths) :]
    rows = table_ref.shape[0] // 3
    tile, inner, length = x_ref.shape
    flat = [out.reshape(width * tile, inner) for out, width in zip(outs, widths)]

    @pl.loop(0, tile // chunk)
    def _(part):
        block = x_ref[pl.ds(chunk * part, chunk)].reshape(chunk * inner, length)
        product = lax.dot_general(
            table_ref[...], block, (((1,), (1,)), ((), ())), preferred_element_type=jnp.float32
        )
        total = product[2 * rows :] + product[rows : 2 * rows] + product[:rows]
        at = 0
        for out, width in zip(flat, widths):
            for j in range(chunk):
                out[pl.ds(chunk * part + j, width, stride=tile), :] = total[
                    at : at + width, j * inner : (j + 1) * inner
                ]
            at += width


def ordered_blocks(array, axis, blocks):
    return jnp.concatenate(
        [lax.dynamic_slice_in_dim(array, block, 1, axis=axis) for block in blocks], axis=axis
    )


def first_transform(spectrum, table, ordered, blocks, first, widths, after):
    members, span_b, span_q, length = spectrum.shape
    groups = ordered.shape[1]
    width = sum(widths)
    if span_q % 128 or span_b % 8:
        chosen = jnp.asarray(table).reshape(length, groups, -1)[:, :, first : first + width]
        chosen = chosen if blocks is None else ordered_blocks(chosen, 1, blocks)
        whole = jnp.einsum("cbqk,ksx->scxbq", spectrum.astype(jnp.float32), chosen, precision=EXACT)
        if blocks is None:
            return whole
        at = np.cumsum([0, *widths])
        return [
            [whole[step, :, at[k] : at[k + 1]] for step in range(groups)] for k in range(len(widths))
        ]
    operand = jnp.asarray(ordered[:, :, first : first + width].reshape(-1, length))
    tile = 16 if span_b % 16 == 0 else 8
    chunk = 8
    while chunk > 2 and operand.shape[0] * chunk * span_q > 2**18:
        chunk //= 2
    if blocks is None:
        parts = [width * groups]
        out_specs = [
            pl.BlockSpec((groups, None, width, tile, span_q), lambda c, b: (0, c, 0, b, 0))
        ]
        out_shape = [jax.ShapeDtypeStruct((groups, members, width, span_b, span_q), jnp.float32)]
    else:
        parts = list(widths) * groups
        out_specs = [
            pl.BlockSpec((None, part, tile, span_q), lambda c, b: (c, 0, b, 0)) for part in parts
        ]
        out_shape = [
            jax.ShapeDtypeStruct((members, part, span_b, span_q), jnp.float32) for part in parts
        ]
    outs = pl.pallas_call(
        functools.partial(first_kernel, widths=parts, chunk=chunk),
        grid=(members, span_b // tile),
        in_specs=[
            pl.BlockSpec(operand.shape, lambda c, b: (0, 0)),
            pl.BlockSpec((None, tile, span_q, length), lambda c, b: (c, b, 0, 0)),
        ]
        + [ANY] * len(after),
        out_specs=out_specs,
        out_shape=out_shape,
        compiler_params=params(),
        cost_estimate=cost(12 + width),
        name="first",
    )(operand, spectrum, *after)
    if blocks is None:
        return outs[0]
    return [outs[k :: len(widths)] for k in range(len(widths))]


def edge_rows(width):
    rows = 8
    while rows < 2 * width:
        rows *= 2
    return rows


def second_kernel(sources_ref, table_ref, *rest, count, planes, span_y):
    ins, out_ref, value_ref = rest[:count], rest[-2], rest[-1]
    tile, span_b, span_q = ins[0].shape
    groups = out_ref.shape[0]
    length = groups * span_y
    first = pl.program_id(1) * tile
    for step in range(count):
        at = pl.multiple_of(sources_ref[step] * span_b, 8)
        for j in range(tile):
            value_ref[pl.ds(at, span_b), j * span_q : (j + 1) * span_q] = ins[step][j]
    parts = value_parts(value_ref[...])
    stacked = jnp.concatenate([parts[p] for p in VALUE_PARTS], axis=0)
    product = jnp.dot(table_ref[...], stacked, preferred_element_type=jnp.float32)

    @pl.when(first == 0)
    def _():
        rest_rows = out_ref.shape[1] - planes * span_y
        out_ref[:, planes * span_y :, :] = jnp.zeros((groups, rest_rows, span_q), jnp.float32)

    for j in range(tile):
        field = product[:, j * span_q : (j + 1) * span_q]
        at = pl.multiple_of((first + j) * span_y, 8)
        out_ref[:, pl.ds(at, span_y), :] = field.reshape(groups, span_y, span_q)
        edge = planes * span_y + 2 * (first + j)
        for g in range(groups):
            before = (g * span_y - 1) % length
            behind = (g + 1) * span_y % length
            out_ref[g, pl.ds(edge, 1), :] = field[before : before + 1]
            out_ref[g, pl.ds(edge + 1, 1), :] = field[behind : behind + 1]


def second_transform(pieces, table, stacked, sources, groups, after):
    count = len(pieces)
    members, width, span_b, span_q = pieces[0].shape
    length = count * span_b
    span_y = length // groups
    edge = edge_rows(width)
    out_shape = (groups, members, width * span_y + edge, span_q)
    if span_q % 128 or span_b % 8 or span_y % 8:
        chosen = ordered_blocks(jnp.asarray(table).reshape(count, span_b, length), 0, sources)
        pieces = jnp.stack([pieces[step] for step in range(count)])
        field = jnp.einsum("scabq,sby->cayq", pieces, chosen, precision=EXACT)
        inner = field.reshape(members, width, groups, span_y, span_q)
        inner = inner.transpose(2, 0, 1, 3, 4).reshape(groups, members, width * span_y, span_q)
        before = jnp.roll(field, 1, axis=2)[:, :, ::span_y]
        behind = jnp.roll(field, -1, axis=2)[:, :, span_y - 1 :: span_y]
        edges = jnp.stack([before, behind], axis=2).transpose(3, 0, 1, 2, 4)
        edges = edges.reshape(groups, members, 2 * width, span_q)
        edges = jnp.pad(edges, ((0, 0), (0, 0), (0, edge - 2 * width), (0, 0)))
        return jnp.concatenate([inner, edges], axis=2)
    tile = 2 if width % 2 == 0 else 1
    if isinstance(pieces, list):
        in_specs = [pl.BlockSpec((None, tile, span_b, span_q), lambda c, a: (c, a, 0, 0))] * count
    else:
        in_specs = [
            pl.BlockSpec((None, None, tile, span_b, span_q), lambda c, a, s=s: (s, c, a, 0, 0))
            for s in range(count)
        ]
        pieces = [pieces] * count
    return pl.pallas_call(
        functools.partial(second_kernel, count=count, planes=width, span_y=span_y),
        grid=(members, width // tile),
        in_specs=[
            pl.BlockSpec(memory_space=pltpu.SMEM),
            pl.BlockSpec(stacked.shape, lambda c, a: (0, 0)),
        ]
        + in_specs
        + [ANY] * len(after),
        out_specs=pl.BlockSpec((groups, None, out_shape[2], span_q), lambda c, a: (0, c, 0, 0)),
        out_shape=jax.ShapeDtypeStruct(out_shape, jnp.float32),
        scratch_shapes=[pltpu.VMEM((length, tile * span_q), jnp.float32)],
        compiler_params=params(),
        cost_estimate=cost(1 + 2 * width),
        name="second",
    )(jnp.stack(sources).astype(jnp.int32), stacked, *pieces, *after)


def third_kernel(table_ref, in_ref, edge_in_ref, *rest):
    out_ref, edge_ref = rest[-2:]
    member = pl.program_id(1)

    def level_of(ref):
        value = jnp.concatenate([ref[g] for g in range(ref.shape[0])], axis=1)
        parts = value_parts(value)
        stacked = jnp.concatenate([parts[p] for p in VALUE_PARTS], axis=1)
        field = jnp.dot(stacked, table_ref[...], preferred_element_type=jnp.float32)
        return 0.5 * (field * field)

    def add(ref, level):
        @pl.when(member == 0)
        def _():
            ref[...] = level

        @pl.when(member > 0)
        def _():
            ref[...] += level

    add(out_ref, level_of(in_ref).reshape(out_ref.shape))

    @pl.when(pl.program_id(0) == 0)
    def _():
        add(edge_ref, level_of(edge_in_ref))


def third_transform(received, width, table, stacked, after):
    groups, members, rows, span_q = received.shape
    edge = edge_rows(width)
    span_y = (rows - edge) // width
    length = groups * span_q
    if span_q % 128 or span_y % 8:
        chosen = jnp.asarray(table).reshape(groups, span_q, length)
        field = jnp.einsum("scrq,sqz->crz", received, chosen, precision=EXACT)
        level = 0.5 * jnp.sum(field * field, axis=0)
        return level[: width * span_y].reshape(width, span_y, length), level[width * span_y :]
    tile = 2 if width % 2 == 0 else 1
    return pl.pallas_call(
        third_kernel,
        grid=(width // tile, members),
        in_specs=[
            pl.BlockSpec(stacked.shape, lambda a, c: (0, 0)),
            pl.BlockSpec((groups, None, tile * span_y, span_q), lambda a, c: (0, c, a, 0)),
            pl.BlockSpec(
                (groups, None, edge, span_q), lambda a, c: (0, c, width * span_y // edge, 0)
            ),
        ]
        + [ANY] * len(after),
        out_specs=[
            pl.BlockSpec((tile, span_y, length), lambda a, c: (a, 0, 0)),
            pl.BlockSpec((edge, length), lambda a, c: (0, 0)),
        ],
        out_shape=[
            jax.ShapeDtypeStruct((width, span_y, length), jnp.float32),
            jax.ShapeDtypeStruct((edge, length), jnp.float32),
        ],
        compiler_params=params(),
        cost_estimate=cost(1 + 2 * width),
        name="third",
    )(stacked, received, received, *after)


def normal_kernel(centre_ref, before_ref, behind_ref, edge_ref, *rest, skip):
    level_ref, normal_ref, token_ref = rest[-3:]
    width, span_y, length = centre_ref.shape
    i = pl.program_id(0) + skip
    centre = centre_ref[i]
    before = jnp.where(i == 0, before_ref[0], centre_ref[jnp.maximum(i - 1, 0)])
    behind = jnp.where(i == width - 1, behind_ref[0], centre_ref[jnp.minimum(i + 1, width - 1)])
    row = lax.broadcasted_iota(jnp.int32, (span_y, length), 0)
    left = jnp.where(row == 0, edge_ref[pl.ds(2 * i, 1), :], pltpu.roll(centre, 1, 0))
    right = jnp.where(
        row == span_y - 1, edge_ref[pl.ds(2 * i + 1, 1), :], pltpu.roll(centre, span_y - 1, 0)
    )
    step_x = 0.5 * (behind - before)
    step_y = 0.5 * (right - left)
    step_z = 0.5 * (pltpu.roll(centre, length - 1, 1) - pltpu.roll(centre, 1, 1))
    magnitude = jnp.sqrt(step_x * step_x + step_y * step_y + step_z * step_z)
    inverse = -1.0 / jnp.maximum(magnitude, 1.0)
    level_ref[0] = centre
    token_ref[...] = jnp.zeros_like(token_ref)
    normal_ref[0, 0] = (step_x * inverse).astype(jnp.bfloat16)
    normal_ref[1, 0] = (step_y * inverse).astype(jnp.bfloat16)
    normal_ref[2, 0] = (step_z * inverse).astype(jnp.bfloat16)


def write_normals(centre, before, behind, edge, skip, count, first, whole, held):
    width, span_y, length = centre.shape
    before, before_at = before
    behind, behind_at = behind
    held = () if held is None else held
    return pl.pallas_call(
        functools.partial(normal_kernel, skip=skip),
        grid=(count,),
        in_specs=[
            pl.BlockSpec((width, span_y, length), lambda i: (0, 0, 0)),
            pl.BlockSpec((1, span_y, length), lambda i: (before_at, 0, 0)),
            pl.BlockSpec((1, span_y, length), lambda i: (behind_at, 0, 0)),
            pl.BlockSpec(edge.shape, lambda i: (0, 0)),
        ]
        + [ANY] * len(held),
        out_specs=[
            pl.BlockSpec((1, span_y, length), lambda i: (first + skip + i, 0, 0)),
            pl.BlockSpec((3, 1, span_y, length), lambda i: (0, first + skip + i, 0, 0)),
            pl.BlockSpec((8, 128), lambda i: (0, 0)),
        ],
        out_shape=[
            jax.ShapeDtypeStruct((whole, span_y, length), jnp.float32),
            jax.ShapeDtypeStruct((3, whole, span_y, length), jnp.bfloat16),
            jax.ShapeDtypeStruct((8, 128), jnp.float32),
        ],
        input_output_aliases={4 + k: k for k in range(len(held))},
        compiler_params=params(),
        cost_estimate=cost(1 + count / 2),
        name="normals",
    )(centre, before, behind, edge, *held)


def slab_widths(planes):
    last = min(LAST, max(planes // 4, 1))
    left = planes - last
    widths = []
    while left:
        width = min(PATTERN[min(len(widths), len(PATTERN) - 1)], left)
        widths.append(width)
        left -= width
    return widths + [last]


def ring(axis, up):
    count = lax.axis_size(axis)
    return [(i, (i + 1) % count if up else (i - 1) % count) for i in range(count)]


def body(spectrum):
    length = spectrum.shape[3]
    rows = lax.axis_size("row")
    cols = lax.axis_size("col")
    planes = length // rows
    table = fourier_table(length)
    parts = table_parts(table)
    first_table = np.stack([part.T.reshape(rows, planes, length) for part in parts])
    second_table = jnp.asarray(np.concatenate([parts[p].T for p in TABLE_PARTS], axis=1))
    third_table = jnp.asarray(np.concatenate([parts[p] for p in TABLE_PARTS], axis=0))

    widths = slab_widths(planes)
    slabs = len(widths)
    split = slabs // 2
    start = planes - sum(widths[:split])
    starts = [(start + sum(widths[:slab])) % planes for slab in range(slabs)]

    me = lax.axis_index("row")
    targets = [partner(me, step, rows) for step in range(rows)]
    sources = [sender(me, step, rows) for step in range(rows)]
    pairs = [[(i, partner(i, step, rows)) for i in range(rows)] for step in range(rows)]
    ordered = ordered_blocks(jnp.asarray(first_table), 1, targets)

    def first(chosen, after):
        outs = first_transform(
            spectrum, table, ordered, targets, starts[chosen[0]], [widths[s] for s in chosen], after
        )
        for slab, out in zip(chosen, outs):
            pieces[slab] = [out[0]] + [
                lax.ppermute(out[step], "row", pairs[step]) for step in range(1, rows)
            ]

    pieces, arrived, levels, edges, halo = {}, {}, {}, {}, {}
    held = None

    def normals(slab, skip=0, count=None):
        nonlocal held
        before = (levels[(slab - 1) % slabs], widths[(slab - 1) % slabs] - 1)
        behind = (levels[(slab + 1) % slabs] if slab + 1 in levels or slab + 1 == slabs else levels[slab], 0)
        if slab == split:
            before = (halo["before"], 0)
        if slab == split - 1:
            behind = (halo["behind"], 0)
        count = widths[slab] - skip if count is None else count
        *held, token = write_normals(
            levels[slab], before, behind, edges[slab], skip, count, starts[slab], planes, held
        )
        return token

    def third(slab, after):
        levels[slab], edges[slab] = third_transform(
            arrived.pop(slab), widths[slab], table, third_table, after
        )
        if slab == split:
            halo["before"] = lax.ppermute(levels[split - 1][-1:], "row", ring("row", True))
            halo["behind"] = lax.ppermute(levels[split][:1], "row", ring("row", False))

    def second(slab, after):
        from_whom = sources if slab else [jnp.int32(step) for step in range(rows)]
        return second_transform(pieces[slab], table, second_table, from_whom, cols, after)

    spectral = first_transform(spectrum, table, first_table, None, starts[0], widths[:1], ())
    pieces[0] = lax.all_to_all(spectral, "row", split_axis=0, concat_axis=0, tiled=True)
    first([1, 2] if split > 2 else [1], (spectral,))
    tokens = {}
    for slab in range(slabs):
        after = [levels[slab - 2]] if slab >= 2 else []
        if slab + 1 < slabs and slab != 1:
            after.append(pieces[slab + 1][0])
        spread = second(slab, after)
        arrived[slab] = lax.all_to_all(spread, "col", split_axis=0, concat_axis=0, tiled=True)
        after = [spread]
        if slab + 2 < slabs and slab + 2 not in pieces:
            first([slab + 2], (pieces[slab + 1][rows - 1],))
            after = [pieces[slab + 2][0]]
        if slab >= 1:
            if slab - 3 in tokens:
                after.append(tokens[slab - 3])
            third(slab - 1, after)
        if slab >= 3:
            tokens[slab - 2] = normals(slab - 2)
    after = [tokens[key] for key in sorted(tokens)[-1:]]
    if widths[slabs - 2] > 1:
        after = [normals(slabs - 2, 0, widths[slabs - 2] - 1)]
    third(slabs - 1, after)
    normals(slabs - 2, widths[slabs - 2] - 1)
    normals(slabs - 1)
    normals(0)
    return tuple(held)


def solution(mesh):
    return jax.shard_map(
        body,
        mesh=mesh,
        in_specs=(P(None, "row", "col", None),),
        out_specs=(P("row", "col", None), P(None, "row", "col", None)),
        check_vma=False,
    )
```

```python
import functools
import math

import jax
import jax.numpy as jnp
import ml_dtypes
import numpy as np
from jax import lax
from jax.experimental import pallas as pl
from jax.experimental.pallas import tpu as pltpu
from jax.sharding import PartitionSpec as P

EXACT = lax.Precision.HIGHEST
TABLE_PARTS = (0, 1, 2, 0, 1, 0)
VALUE_PARTS = (0, 0, 0, 1, 1, 2)
VMEM_BYTES = 48 * 1024 * 1024
SCALE = 1.0
PATTERN = (6, 6, 10, 10, 16, 12)
LAST = 4


def fourier_table(length):
    wave_number = np.arange(length)[:, None]
    position = np.arange(length)[None, :]
    nyquist = length // 2
    frequency = np.where(wave_number <= nyquist, wave_number, wave_number - nyquist)
    angle = (frequency * position % length) * (2.0 * math.pi / length)
    edge = (wave_number == 0) | (wave_number == nyquist)
    weight = np.where(edge, math.sqrt(1.0 / length), math.sqrt(2.0 / length))
    table = np.where(wave_number <= nyquist, np.cos(angle), np.sin(angle)) * weight
    return table.astype(np.float32)


def table_parts(table):
    parts = []
    rest = table
    for _ in range(3):
        part = rest.astype(ml_dtypes.bfloat16)
        parts.append(part)
        rest = rest - part.astype(np.float32)
    return parts


def value_parts(value):
    high = value.astype(jnp.bfloat16)
    rest = value - high.astype(jnp.float32)
    middle = rest.astype(jnp.bfloat16)
    low = (rest - middle.astype(jnp.float32)).astype(jnp.bfloat16)
    return high, middle, low


def partner(me, step, count):
    if count & (count - 1) == 0:
        return me ^ step
    return (me + step) % count


def sender(me, step, count):
    if count & (count - 1) == 0:
        return me ^ step
    return (me + count - step) % count


ANY = pl.BlockSpec(memory_space=pl.ANY)


def cost(time):
    return pl.CostEstimate(flops=0, bytes_accessed=int(SCALE * time * 3.0e6), transcendentals=0)


def params():
    return pltpu.CompilerParams(vmem_limit_bytes=VMEM_BYTES)


def first_kernel(table_ref, x_ref, *rest, widths, chunk):
    outs = rest[-len(widths) :]
    rows = table_ref.shape[0] // 3
    tile, inner, length = x_ref.shape
    flat = [out.reshape(width * tile, inner) for out, width in zip(outs, widths)]

    @pl.loop(0, tile // chunk)
    def _(part):
        block = x_ref[pl.ds(chunk * part, chunk)].reshape(chunk * inner, length)
        product = lax.dot_general(
            table_ref[...], block, (((1,), (1,)), ((), ())), preferred_element_type=jnp.float32
        )
        total = product[2 * rows :] + product[rows : 2 * rows] + product[:rows]
        at = 0
        for out, width in zip(flat, widths):
            for j in range(chunk):
                out[pl.ds(chunk * part + j, width, stride=tile), :] = total[
                    at : at + width, j * inner : (j + 1) * inner
                ]
            at += width


def ordered_blocks(array, axis, blocks):
    return jnp.concatenate(
        [lax.dynamic_slice_in_dim(array, block, 1, axis=axis) for block in blocks], axis=axis
    )


def first_transform(spectrum, table, ordered, blocks, chosen_members, first, width, after):
    _, span_b, span_q, length = spectrum.shape
    member, members = chosen_members.start, len(chosen_members)
    groups = ordered.shape[1]
    if span_q % 128 or span_b % 8:
        part = spectrum[member : member + members].astype(jnp.float32)
        chosen = jnp.asarray(table).reshape(length, groups, -1)[:, :, first : first + width]
        chosen = chosen if blocks is None else ordered_blocks(chosen, 1, blocks)
        whole = jnp.einsum("cbqk,ksx->scxbq", part, chosen, precision=EXACT)
        return whole if blocks is None else [whole[step] for step in range(groups)]
    operand = jnp.asarray(ordered[:, :, first : first + width].reshape(-1, length))
    tile = 16 if span_b % 16 == 0 else 8
    chunk = 8
    while chunk > 2 and operand.shape[0] * chunk * span_q > 2**18:
        chunk //= 2
    if blocks is None:
        parts = [width * groups]
        out_specs = [
            pl.BlockSpec((groups, None, width, tile, span_q), lambda c, b: (0, c, 0, b, 0))
        ]
        out_shape = [jax.ShapeDtypeStruct((groups, members, width, span_b, span_q), jnp.float32)]
    else:
        parts = [width] * groups
        out_specs = [pl.BlockSpec((None, width, tile, span_q), lambda c, b: (c, 0, b, 0))] * groups
        out_shape = [
            jax.ShapeDtypeStruct((members, width, span_b, span_q), jnp.float32)
        ] * groups
    outs = pl.pallas_call(
        functools.partial(first_kernel, widths=parts, chunk=chunk),
        grid=(members, span_b // tile),
        in_specs=[
            pl.BlockSpec(operand.shape, lambda c, b: (0, 0)),
            pl.BlockSpec((None, tile, span_q, length), lambda c, b: (member + c, b, 0, 0)),
        ]
        + [ANY] * len(after),
        out_specs=out_specs,
        out_shape=out_shape,
        compiler_params=params(),
        cost_estimate=cost(12 + width),
        name="first",
    )(operand, spectrum, *after)
    return outs[0] if blocks is None else outs


def edge_rows(width):
    rows = 8
    while rows < 2 * width:
        rows *= 2
    return rows


def second_kernel(sources_ref, table_ref, *rest, count, planes, span_y):
    ins, out_ref, value_ref = rest[:count], rest[-2], rest[-1]
    tile, span_b, span_q = ins[0].shape
    groups = out_ref.shape[0]
    length = groups * span_y
    first = pl.program_id(1) * tile
    for step in range(count):
        at = pl.multiple_of(sources_ref[step] * span_b, 8)
        for j in range(tile):
            value_ref[pl.ds(at, span_b), j * span_q : (j + 1) * span_q] = ins[step][j]
    parts = value_parts(value_ref[...])
    stacked = jnp.concatenate([parts[p] for p in VALUE_PARTS], axis=0)
    product = jnp.dot(table_ref[...], stacked, preferred_element_type=jnp.float32)

    @pl.when(first == 0)
    def _():
        rest_rows = out_ref.shape[1] - planes * span_y
        out_ref[:, planes * span_y :, :] = jnp.zeros((groups, rest_rows, span_q), jnp.float32)

    for j in range(tile):
        field = product[:, j * span_q : (j + 1) * span_q]
        at = pl.multiple_of((first + j) * span_y, 8)
        out_ref[:, pl.ds(at, span_y), :] = field.reshape(groups, span_y, span_q)
        edge = planes * span_y + 2 * (first + j)
        for g in range(groups):
            before = (g * span_y - 1) % length
            behind = (g + 1) * span_y % length
            out_ref[g, pl.ds(edge, 1), :] = field[before : before + 1]
            out_ref[g, pl.ds(edge + 1, 1), :] = field[behind : behind + 1]


def second_transform(pieces, table, stacked, sources, groups, after):
    count = len(pieces)
    members, width, span_b, span_q = pieces[0].shape
    length = count * span_b
    span_y = length // groups
    edge = edge_rows(width)
    out_shape = (groups, members, width * span_y + edge, span_q)
    if span_q % 128 or span_b % 8 or span_y % 8:
        chosen = ordered_blocks(jnp.asarray(table).reshape(count, span_b, length), 0, sources)
        pieces = jnp.stack([pieces[step] for step in range(count)])
        field = jnp.einsum("scabq,sby->cayq", pieces, chosen, precision=EXACT)
        inner = field.reshape(members, width, groups, span_y, span_q)
        inner = inner.transpose(2, 0, 1, 3, 4).reshape(groups, members, width * span_y, span_q)
        before = jnp.roll(field, 1, axis=2)[:, :, ::span_y]
        behind = jnp.roll(field, -1, axis=2)[:, :, span_y - 1 :: span_y]
        edges = jnp.stack([before, behind], axis=2).transpose(3, 0, 1, 2, 4)
        edges = edges.reshape(groups, members, 2 * width, span_q)
        edges = jnp.pad(edges, ((0, 0), (0, 0), (0, edge - 2 * width), (0, 0)))
        return jnp.concatenate([inner, edges], axis=2)
    tile = 2 if width % 2 == 0 else 1
    if isinstance(pieces, list):
        in_specs = [pl.BlockSpec((None, tile, span_b, span_q), lambda c, a: (c, a, 0, 0))] * count
    else:
        in_specs = [
            pl.BlockSpec((None, None, tile, span_b, span_q), lambda c, a, s=s: (s, c, a, 0, 0))
            for s in range(count)
        ]
        pieces = [pieces] * count
    return pl.pallas_call(
        functools.partial(second_kernel, count=count, planes=width, span_y=span_y),
        grid=(members, width // tile),
        in_specs=[
            pl.BlockSpec(memory_space=pltpu.SMEM),
            pl.BlockSpec(stacked.shape, lambda c, a: (0, 0)),
        ]
        + in_specs
        + [ANY] * len(after),
        out_specs=pl.BlockSpec((groups, None, out_shape[2], span_q), lambda c, a: (0, c, 0, 0)),
        out_shape=jax.ShapeDtypeStruct(out_shape, jnp.float32),
        scratch_shapes=[pltpu.VMEM((length, tile * span_q), jnp.float32)],
        compiler_params=params(),
        cost_estimate=cost(1 + 2 * width),
        name="second",
    )(jnp.stack(sources).astype(jnp.int32), stacked, *pieces, *after)


def third_kernel(table_ref, *rest, firsts, together):
    out_ref, edge_ref = rest[-2:]
    ins, edge_ins = rest[: len(firsts)], rest[len(firsts) : 2 * len(firsts)]
    member = pl.program_id(1)

    def value_of(refs):
        value = None
        for ref, first in zip(refs, firsts):
            here = jnp.concatenate([ref[g] for g in range(ref.shape[0])], axis=1)
            value = here if value is None else jnp.where(member >= first, here, value)
        return value

    def level_of(value):
        parts = value_parts(value)
        stacked = jnp.concatenate([parts[p] for p in VALUE_PARTS], axis=1)
        field = jnp.dot(stacked, table_ref[...], preferred_element_type=jnp.float32)
        return 0.5 * (field * field)

    def add(ref, level):
        @pl.when(member == 0)
        def _():
            ref[...] = level

        @pl.when(member > 0)
        def _():
            ref[...] += level

    if together:
        level = level_of(jnp.concatenate([value_of(ins), value_of(edge_ins)], axis=0))
        rows = level.shape[0] - edge_ref.shape[0]
        add(out_ref, level[:rows].reshape(out_ref.shape))
        add(edge_ref, level[rows:])
        return
    add(out_ref, level_of(value_of(ins)).reshape(out_ref.shape))

    @pl.when(pl.program_id(0) == 0)
    def _():
        add(edge_ref, level_of(value_of(edge_ins)))


def third_transform(received, width, table, stacked, after):
    groups, _, rows, span_q = received[0].shape
    edge = edge_rows(width)
    span_y = (rows - edge) // width
    length = groups * span_q
    if span_q % 128 or span_y % 8:
        chosen = jnp.asarray(table).reshape(groups, span_q, length)
        received = jnp.concatenate(received, axis=1)
        field = jnp.einsum("scrq,sqz->crz", received, chosen, precision=EXACT)
        level = 0.5 * jnp.sum(field * field, axis=0)
        return level[: width * span_y].reshape(width, span_y, length), level[width * span_y :]
    tile = 4 if width == 4 else 2 if width % 2 == 0 else 1
    counts = [array.shape[1] for array in received]
    firsts = [sum(counts[:k]) for k in range(len(counts))]

    def spec(block_rows, block_of, first, count):
        return pl.BlockSpec(
            (groups, None, block_rows, span_q),
            lambda a, c: (0, jnp.clip(c - first, 0, count - 1), block_of(a), 0),
        )

    return pl.pallas_call(
        functools.partial(third_kernel, firsts=firsts, together=width == tile),
        grid=(width // tile, sum(counts)),
        in_specs=[pl.BlockSpec(stacked.shape, lambda a, c: (0, 0))]
        + [spec(tile * span_y, lambda a: a, *one) for one in zip(firsts, counts)]
        + [spec(edge, lambda a: width * span_y // edge, *one) for one in zip(firsts, counts)]
        + [ANY] * len(after),
        out_specs=[
            pl.BlockSpec((tile, span_y, length), lambda a, c: (a, 0, 0)),
            pl.BlockSpec((edge, length), lambda a, c: (0, 0)),
        ],
        out_shape=[
            jax.ShapeDtypeStruct((width, span_y, length), jnp.float32),
            jax.ShapeDtypeStruct((edge, length), jnp.float32),
        ],
        compiler_params=params(),
        cost_estimate=cost(1 + 2 * width),
        name="third",
    )(stacked, *received, *received, *after)


def normal_kernel(centre_ref, before_ref, behind_ref, edge_ref, *rest, skip):
    level_ref, normal_ref, token_ref = rest[-3:]
    width, span_y, length = centre_ref.shape
    i = pl.program_id(0) + skip
    centre = centre_ref[i]
    before = jnp.where(i == 0, before_ref[0], centre_ref[jnp.maximum(i - 1, 0)])
    behind = jnp.where(i == width - 1, behind_ref[0], centre_ref[jnp.minimum(i + 1, width - 1)])
    row = lax.broadcasted_iota(jnp.int32, (span_y, length), 0)
    left = jnp.where(row == 0, edge_ref[pl.ds(2 * i, 1), :], pltpu.roll(centre, 1, 0))
    right = jnp.where(
        row == span_y - 1, edge_ref[pl.ds(2 * i + 1, 1), :], pltpu.roll(centre, span_y - 1, 0)
    )
    step_x = 0.5 * (behind - before)
    step_y = 0.5 * (right - left)
    step_z = 0.5 * (pltpu.roll(centre, length - 1, 1) - pltpu.roll(centre, 1, 1))
    magnitude = jnp.sqrt(step_x * step_x + step_y * step_y + step_z * step_z)
    inverse = -1.0 / jnp.maximum(magnitude, 1.0)
    level_ref[0] = centre
    token_ref[...] = jnp.zeros_like(token_ref)
    normal_ref[0, 0] = (step_x * inverse).astype(jnp.bfloat16)
    normal_ref[1, 0] = (step_y * inverse).astype(jnp.bfloat16)
    normal_ref[2, 0] = (step_z * inverse).astype(jnp.bfloat16)


def write_normals(centre, before, behind, edge, skip, count, first, whole, held):
    width, span_y, length = centre.shape
    before, before_at = before
    behind, behind_at = behind
    held = () if held is None else held
    return pl.pallas_call(
        functools.partial(normal_kernel, skip=skip),
        grid=(count,),
        in_specs=[
            pl.BlockSpec((width, span_y, length), lambda i: (0, 0, 0)),
            pl.BlockSpec((1, span_y, length), lambda i: (before_at, 0, 0)),
            pl.BlockSpec((1, span_y, length), lambda i: (behind_at, 0, 0)),
            pl.BlockSpec(edge.shape, lambda i: (0, 0)),
        ]
        + [ANY] * len(held),
        out_specs=[
            pl.BlockSpec((1, span_y, length), lambda i: (first + skip + i, 0, 0)),
            pl.BlockSpec((3, 1, span_y, length), lambda i: (0, first + skip + i, 0, 0)),
            pl.BlockSpec((8, 128), lambda i: (0, 0)),
        ],
        out_shape=[
            jax.ShapeDtypeStruct((whole, span_y, length), jnp.float32),
            jax.ShapeDtypeStruct((3, whole, span_y, length), jnp.bfloat16),
            jax.ShapeDtypeStruct((8, 128), jnp.float32),
        ],
        input_output_aliases={4 + k: k for k in range(len(held))},
        compiler_params=params(),
        cost_estimate=cost(1 + count / 2),
        name="normals",
    )(centre, before, behind, edge, *held)


def slab_widths(planes):
    last = min(LAST, max(planes // 4, 1))
    left = planes - last
    widths = []
    while left:
        width = min(PATTERN[min(len(widths), len(PATTERN) - 1)], left)
        widths.append(width)
        left -= width
    return widths + [last]


def ring(axis, up):
    count = lax.axis_size(axis)
    return [(i, (i + 1) % count if up else (i - 1) % count) for i in range(count)]


def body(spectrum):
    length = spectrum.shape[3]
    rows = lax.axis_size("row")
    cols = lax.axis_size("col")
    planes = length // rows
    table = fourier_table(length)
    parts = table_parts(table)
    first_table = np.stack([part.T.reshape(rows, planes, length) for part in parts])
    second_table = jnp.asarray(np.concatenate([parts[p].T for p in TABLE_PARTS], axis=1))
    third_table = jnp.asarray(np.concatenate([parts[p] for p in TABLE_PARTS], axis=0))

    widths = slab_widths(planes)
    slabs = len(widths)
    split = slabs // 2
    start = planes - sum(widths[:split])
    starts = [(start + sum(widths[:slab])) % planes for slab in range(slabs)]

    me = lax.axis_index("row")
    targets = [partner(me, step, rows) for step in range(rows)]
    sources = [sender(me, step, rows) for step in range(rows)]
    pairs = [[(i, partner(i, step, rows)) for i in range(rows)] for step in range(rows)]
    ordered = ordered_blocks(jnp.asarray(first_table), 1, targets)

    members = spectrum.shape[0]
    parts = [(0, range(0, 1)), (0, range(1, members))]
    parts += [(slab, range(0, members)) for slab in range(1, slabs)]

    def first(part, after):
        slab, chosen = parts[part]
        outs = first_transform(
            spectrum, table, ordered, targets, chosen, starts[slab], widths[slab], after
        )
        pieces[part] = [outs[0]] + [
            lax.ppermute(outs[step], "row", pairs[step]) for step in range(1, rows)
        ]

    pieces, arrived, levels, edges, halo = {}, {}, {}, {}, {}
    held = None

    def normals(slab, skip=0, count=None):
        nonlocal held
        before_slab, behind_slab = (slab - 1) % slabs, (slab + 1) % slabs
        before = (levels[before_slab], widths[before_slab] - 1) if before_slab in levels else (levels[slab], 0)
        behind = (levels[behind_slab], 0) if behind_slab in levels else (levels[slab], 0)
        if slab == split:
            before = (halo["before"], 0)
        if slab == split - 1:
            behind = (halo["behind"], 0)
        count = widths[slab] - skip if count is None else count
        *held, token = write_normals(
            levels[slab], before, behind, edges[slab], skip, count, starts[slab], planes, held
        )
        return token

    def third(slab, after):
        received = [arrived[part] for part in range(len(parts)) if parts[part][0] == slab]
        levels[slab], edges[slab] = third_transform(
            received, widths[slab], table, third_table, after
        )
        if slab == split:
            halo["before"] = lax.ppermute(levels[split - 1][-1:], "row", ring("row", True))
            halo["behind"] = lax.ppermute(levels[split][:1], "row", ring("row", False))

    def second(part, after):
        from_whom = sources if part else [jnp.int32(step) for step in range(rows)]
        return second_transform(pieces[part], table, second_table, from_whom, cols, after)

    spectral = first_transform(
        spectrum, table, first_table, None, parts[0][1], starts[0], widths[0], ()
    )
    pieces[0] = lax.all_to_all(spectral, "row", split_axis=0, concat_axis=0, tiled=True)
    first(1, (spectral,))
    tokens = {}
    for part in range(len(parts)):
        after = []
        if part >= 2:
            after.append(levels[part - 3] if part >= 3 else arrived[0])
        if part + 1 < len(parts):
            after.append(pieces[part + 1][0])
        spread = second(part, after)
        arrived[part] = lax.all_to_all(spread, "col", split_axis=0, concat_axis=0, tiled=True)
        after = [spread]
        if part + 2 < len(parts):
            first(part + 2, (pieces[part + 1][rows - 1],))
            after = [pieces[part + 2][0]]
        if part >= 2:
            slab = part - 2
            if slab - 2 in tokens:
                after.append(tokens[slab - 2])
            third(slab, after)
            if slab >= 2:
                tokens[slab - 1] = normals(slab - 1)
            elif slab == 1 and widths[0] > 1:
                tokens[0] = normals(0, 1)
    after = [tokens[key] for key in sorted(tokens)[-1:]]
    if widths[slabs - 2] > 1:
        after = [normals(slabs - 2, 0, widths[slabs - 2] - 1)]
    third(slabs - 1, after)
    normals(slabs - 2, widths[slabs - 2] - 1)
    normals(slabs - 1)
    normals(0, 0, 1)
    return tuple(held)


def solution(mesh):
    return jax.shard_map(
        body,
        mesh=mesh,
        in_specs=(P(None, "row", "col", None),),
        out_specs=(P("row", "col", None), P(None, "row", "col", None)),
        check_vma=False,
    )
```

```python
import functools
import math

import jax
import jax.numpy as jnp
import ml_dtypes
import numpy as np
from jax import lax
from jax.experimental import pallas as pl
from jax.experimental.pallas import tpu as pltpu
from jax.sharding import PartitionSpec as P

EXACT = lax.Precision.HIGHEST
TABLE_PARTS = (0, 1, 2, 0, 1, 0)
VALUE_PARTS = (0, 0, 0, 1, 1, 2)
VMEM_BYTES = 48 * 1024 * 1024
SCALE = 1.0
PATTERN = (6, 6, 10, 16, 22)
LAST = 4


def fourier_table(length):
    wave_number = np.arange(length)[:, None]
    position = np.arange(length)[None, :]
    nyquist = length // 2
    frequency = np.where(wave_number <= nyquist, wave_number, wave_number - nyquist)
    angle = (frequency * position % length) * (2.0 * math.pi / length)
    edge = (wave_number == 0) | (wave_number == nyquist)
    weight = np.where(edge, math.sqrt(1.0 / length), math.sqrt(2.0 / length))
    table = np.where(wave_number <= nyquist, np.cos(angle), np.sin(angle)) * weight
    return table.astype(np.float32)


def table_parts(table):
    parts = []
    rest = table
    for _ in range(3):
        part = rest.astype(ml_dtypes.bfloat16)
        parts.append(part)
        rest = rest - part.astype(np.float32)
    return parts


def value_parts(value):
    high = value.astype(jnp.bfloat16)
    rest = value - high.astype(jnp.float32)
    middle = rest.astype(jnp.bfloat16)
    low = (rest - middle.astype(jnp.float32)).astype(jnp.bfloat16)
    return high, middle, low


def partner(me, step, count):
    if count & (count - 1) == 0:
        return me ^ step
    return (me + step) % count


def sender(me, step, count):
    if count & (count - 1) == 0:
        return me ^ step
    return (me + count - step) % count


ANY = pl.BlockSpec(memory_space=pl.ANY)


def cost(time):
    return pl.CostEstimate(flops=0, bytes_accessed=int(SCALE * time * 3.0e6), transcendentals=0)


def params():
    return pltpu.CompilerParams(vmem_limit_bytes=VMEM_BYTES)


def first_kernel(table_ref, x_ref, *rest, widths, chunk):
    outs = rest[-len(widths) :]
    rows = table_ref.shape[0] // 3
    tile, inner, length = x_ref.shape
    flat = [out.reshape(width * tile, inner) for out, width in zip(outs, widths)]

    @pl.loop(0, tile // chunk)
    def _(part):
        block = x_ref[pl.ds(chunk * part, chunk)].reshape(chunk * inner, length)
        product = lax.dot_general(
            table_ref[...], block, (((1,), (1,)), ((), ())), preferred_element_type=jnp.float32
        )
        total = product[2 * rows :] + product[rows : 2 * rows] + product[:rows]
        at = 0
        for out, width in zip(flat, widths):
            for j in range(chunk):
                out[pl.ds(chunk * part + j, width, stride=tile), :] = total[
                    at : at + width, j * inner : (j + 1) * inner
                ]
            at += width


def ordered_blocks(array, axis, blocks):
    return jnp.concatenate(
        [lax.dynamic_slice_in_dim(array, block, 1, axis=axis) for block in blocks], axis=axis
    )


def first_transform(spectrum, table, ordered, blocks, chosen_members, first, width, after):
    _, span_b, span_q, length = spectrum.shape
    member, members = chosen_members.start, len(chosen_members)
    groups = ordered.shape[1]
    if span_q % 128 or span_b % 8:
        part = spectrum[member : member + members].astype(jnp.float32)
        chosen = jnp.asarray(table).reshape(length, groups, -1)[:, :, first : first + width]
        chosen = chosen if blocks is None else ordered_blocks(chosen, 1, blocks)
        whole = jnp.einsum("cbqk,ksx->scxbq", part, chosen, precision=EXACT)
        return whole if blocks is None else [whole[step] for step in range(groups)]
    operand = jnp.asarray(ordered[:, :, first : first + width].reshape(-1, length))
    tile = 16 if span_b % 16 == 0 else 8
    chunk = 8
    while chunk > 2 and operand.shape[0] * chunk * span_q > 2**18:
        chunk //= 2
    if blocks is None:
        parts = [width * groups]
        out_specs = [
            pl.BlockSpec((groups, None, width, tile, span_q), lambda c, b: (0, c, 0, b, 0))
        ]
        out_shape = [jax.ShapeDtypeStruct((groups, members, width, span_b, span_q), jnp.float32)]
    else:
        parts = [width] * groups
        out_specs = [pl.BlockSpec((None, width, tile, span_q), lambda c, b: (c, 0, b, 0))] * groups
        out_shape = [
            jax.ShapeDtypeStruct((members, width, span_b, span_q), jnp.float32)
        ] * groups
    outs = pl.pallas_call(
        functools.partial(first_kernel, widths=parts, chunk=chunk),
        grid=(members, span_b // tile),
        in_specs=[
            pl.BlockSpec(operand.shape, lambda c, b: (0, 0)),
            pl.BlockSpec((None, tile, span_q, length), lambda c, b: (member + c, b, 0, 0)),
        ]
        + [ANY] * len(after),
        out_specs=out_specs,
        out_shape=out_shape,
        compiler_params=params(),
        cost_estimate=cost(12 + width),
        name="first",
    )(operand, spectrum, *after)
    return outs[0] if blocks is None else outs


def edge_rows(width):
    rows = 8
    while rows < 2 * width:
        rows *= 2
    return rows


def second_kernel(sources_ref, table_ref, *rest, count, planes, span_y):
    ins, out_ref, value_ref = rest[:count], rest[-2], rest[-1]
    tile, span_b, span_q = ins[0].shape
    groups = out_ref.shape[0]
    length = groups * span_y
    first = pl.program_id(1) * tile
    for step in range(count):
        at = pl.multiple_of(sources_ref[step] * span_b, 8)
        for j in range(tile):
            value_ref[pl.ds(at, span_b), j * span_q : (j + 1) * span_q] = ins[step][j]
    parts = value_parts(value_ref[...])
    stacked = jnp.concatenate([parts[p] for p in VALUE_PARTS], axis=0)
    product = jnp.dot(table_ref[...], stacked, preferred_element_type=jnp.float32)

    @pl.when(first == 0)
    def _():
        rest_rows = out_ref.shape[1] - planes * span_y
        out_ref[:, planes * span_y :, :] = jnp.zeros((groups, rest_rows, span_q), jnp.float32)

    for j in range(tile):
        field = product[:, j * span_q : (j + 1) * span_q]
        at = pl.multiple_of((first + j) * span_y, 8)
        out_ref[:, pl.ds(at, span_y), :] = field.reshape(groups, span_y, span_q)
        edge = planes * span_y + 2 * (first + j)
        for g in range(groups):
            before = (g * span_y - 1) % length
            behind = (g + 1) * span_y % length
            out_ref[g, pl.ds(edge, 1), :] = field[before : before + 1]
            out_ref[g, pl.ds(edge + 1, 1), :] = field[behind : behind + 1]


def second_transform(pieces, table, stacked, sources, groups, after):
    count = len(pieces)
    members, width, span_b, span_q = pieces[0].shape
    length = count * span_b
    span_y = length // groups
    edge = edge_rows(width)
    out_shape = (groups, members, width * span_y + edge, span_q)
    if span_q % 128 or span_b % 8 or span_y % 8:
        chosen = ordered_blocks(jnp.asarray(table).reshape(count, span_b, length), 0, sources)
        pieces = jnp.stack([pieces[step] for step in range(count)])
        field = jnp.einsum("scabq,sby->cayq", pieces, chosen, precision=EXACT)
        inner = field.reshape(members, width, groups, span_y, span_q)
        inner = inner.transpose(2, 0, 1, 3, 4).reshape(groups, members, width * span_y, span_q)
        before = jnp.roll(field, 1, axis=2)[:, :, ::span_y]
        behind = jnp.roll(field, -1, axis=2)[:, :, span_y - 1 :: span_y]
        edges = jnp.stack([before, behind], axis=2).transpose(3, 0, 1, 2, 4)
        edges = edges.reshape(groups, members, 2 * width, span_q)
        edges = jnp.pad(edges, ((0, 0), (0, 0), (0, edge - 2 * width), (0, 0)))
        return jnp.concatenate([inner, edges], axis=2)
    tile = 2 if width % 2 == 0 else 1
    if isinstance(pieces, list):
        in_specs = [pl.BlockSpec((None, tile, span_b, span_q), lambda c, a: (c, a, 0, 0))] * count
    else:
        in_specs = [
            pl.BlockSpec((None, None, tile, span_b, span_q), lambda c, a, s=s: (s, c, a, 0, 0))
            for s in range(count)
        ]
        pieces = [pieces] * count
    return pl.pallas_call(
        functools.partial(second_kernel, count=count, planes=width, span_y=span_y),
        grid=(members, width // tile),
        in_specs=[
            pl.BlockSpec(memory_space=pltpu.SMEM),
            pl.BlockSpec(stacked.shape, lambda c, a: (0, 0)),
        ]
        + in_specs
        + [ANY] * len(after),
        out_specs=pl.BlockSpec((groups, None, out_shape[2], span_q), lambda c, a: (0, c, 0, 0)),
        out_shape=jax.ShapeDtypeStruct(out_shape, jnp.float32),
        scratch_shapes=[pltpu.VMEM((length, tile * span_q), jnp.float32)],
        compiler_params=params(),
        cost_estimate=cost(1 + 2 * width),
        name="second",
    )(jnp.stack(sources).astype(jnp.int32), stacked, *pieces, *after)


def third_kernel(table_ref, *rest, firsts, together):
    out_ref, edge_ref = rest[-2:]
    ins, edge_ins = rest[: len(firsts)], rest[len(firsts) : 2 * len(firsts)]
    member = pl.program_id(1)

    def value_of(refs):
        value = None
        for ref, first in zip(refs, firsts):
            here = jnp.concatenate([ref[g] for g in range(ref.shape[0])], axis=1)
            value = here if value is None else jnp.where(member >= first, here, value)
        return value

    def level_of(value):
        parts = value_parts(value)
        stacked = jnp.concatenate([parts[p] for p in VALUE_PARTS], axis=1)
        field = jnp.dot(stacked, table_ref[...], preferred_element_type=jnp.float32)
        return 0.5 * (field * field)

    def add(ref, level):
        @pl.when(member == 0)
        def _():
            ref[...] = level

        @pl.when(member > 0)
        def _():
            ref[...] += level

    if together:
        level = level_of(jnp.concatenate([value_of(ins), value_of(edge_ins)], axis=0))
        rows = level.shape[0] - edge_ref.shape[0]
        add(out_ref, level[:rows].reshape(out_ref.shape))
        add(edge_ref, level[rows:])
        return
    add(out_ref, level_of(value_of(ins)).reshape(out_ref.shape))

    @pl.when(pl.program_id(0) == 0)
    def _():
        add(edge_ref, level_of(value_of(edge_ins)))


def third_transform(received, width, table, stacked, after):
    groups, _, rows, span_q = received[0].shape
    edge = edge_rows(width)
    span_y = (rows - edge) // width
    length = groups * span_q
    if span_q % 128 or span_y % 8:
        chosen = jnp.asarray(table).reshape(groups, span_q, length)
        received = jnp.concatenate(received, axis=1)
        field = jnp.einsum("scrq,sqz->crz", received, chosen, precision=EXACT)
        level = 0.5 * jnp.sum(field * field, axis=0)
        return level[: width * span_y].reshape(width, span_y, length), level[width * span_y :]
    tile = 4 if width == 4 else 2 if width % 2 == 0 else 1
    counts = [array.shape[1] for array in received]
    firsts = [sum(counts[:k]) for k in range(len(counts))]

    def spec(block_rows, block_of, first, count):
        return pl.BlockSpec(
            (groups, None, block_rows, span_q),
            lambda a, c: (0, jnp.clip(c - first, 0, count - 1), block_of(a), 0),
        )

    return pl.pallas_call(
        functools.partial(third_kernel, firsts=firsts, together=width == tile),
        grid=(width // tile, sum(counts)),
        in_specs=[pl.BlockSpec(stacked.shape, lambda a, c: (0, 0))]
        + [spec(tile * span_y, lambda a: a, *one) for one in zip(firsts, counts)]
        + [spec(edge, lambda a: width * span_y // edge, *one) for one in zip(firsts, counts)]
        + [ANY] * len(after),
        out_specs=[
            pl.BlockSpec((tile, span_y, length), lambda a, c: (a, 0, 0)),
            pl.BlockSpec((edge, length), lambda a, c: (0, 0)),
        ],
        out_shape=[
            jax.ShapeDtypeStruct((width, span_y, length), jnp.float32),
            jax.ShapeDtypeStruct((edge, length), jnp.float32),
        ],
        compiler_params=params(),
        cost_estimate=cost(1 + 2 * width),
        name="third",
    )(stacked, *received, *received, *after)


def normal_kernel(centre_ref, before_ref, behind_ref, edge_ref, *rest, skip):
    level_ref, normal_ref, token_ref = rest[-3:]
    width, span_y, length = centre_ref.shape
    i = pl.program_id(0) + skip
    centre = centre_ref[i]
    before = jnp.where(i == 0, before_ref[0], centre_ref[jnp.maximum(i - 1, 0)])
    behind = jnp.where(i == width - 1, behind_ref[0], centre_ref[jnp.minimum(i + 1, width - 1)])
    row = lax.broadcasted_iota(jnp.int32, (span_y, length), 0)
    left = jnp.where(row == 0, edge_ref[pl.ds(2 * i, 1), :], pltpu.roll(centre, 1, 0))
    right = jnp.where(
        row == span_y - 1, edge_ref[pl.ds(2 * i + 1, 1), :], pltpu.roll(centre, span_y - 1, 0)
    )
    step_x = 0.5 * (behind - before)
    step_y = 0.5 * (right - left)
    step_z = 0.5 * (pltpu.roll(centre, length - 1, 1) - pltpu.roll(centre, 1, 1))
    magnitude = jnp.sqrt(step_x * step_x + step_y * step_y + step_z * step_z)
    inverse = -1.0 / jnp.maximum(magnitude, 1.0)
    level_ref[0] = centre
    token_ref[...] = jnp.zeros_like(token_ref)
    normal_ref[0, 0] = (step_x * inverse).astype(jnp.bfloat16)
    normal_ref[1, 0] = (step_y * inverse).astype(jnp.bfloat16)
    normal_ref[2, 0] = (step_z * inverse).astype(jnp.bfloat16)


def write_normals(centre, before, behind, edge, skip, count, first, whole, held):
    width, span_y, length = centre.shape
    before, before_at = before
    behind, behind_at = behind
    held = () if held is None else held
    return pl.pallas_call(
        functools.partial(normal_kernel, skip=skip),
        grid=(count,),
        in_specs=[
            pl.BlockSpec((width, span_y, length), lambda i: (0, 0, 0)),
            pl.BlockSpec((1, span_y, length), lambda i: (before_at, 0, 0)),
            pl.BlockSpec((1, span_y, length), lambda i: (behind_at, 0, 0)),
            pl.BlockSpec(edge.shape, lambda i: (0, 0)),
        ]
        + [ANY] * len(held),
        out_specs=[
            pl.BlockSpec((1, span_y, length), lambda i: (first + skip + i, 0, 0)),
            pl.BlockSpec((3, 1, span_y, length), lambda i: (0, first + skip + i, 0, 0)),
            pl.BlockSpec((8, 128), lambda i: (0, 0)),
        ],
        out_shape=[
            jax.ShapeDtypeStruct((whole, span_y, length), jnp.float32),
            jax.ShapeDtypeStruct((3, whole, span_y, length), jnp.bfloat16),
            jax.ShapeDtypeStruct((8, 128), jnp.float32),
        ],
        input_output_aliases={4 + k: k for k in range(len(held))},
        compiler_params=params(),
        cost_estimate=cost(1 + count / 2),
        name="normals",
    )(centre, before, behind, edge, *held)


def slab_widths(planes):
    last = min(LAST, max(planes // 4, 1))
    left = planes - last
    widths = []
    while left:
        width = min(PATTERN[min(len(widths), len(PATTERN) - 1)], left)
        widths.append(width)
        left -= width
    return widths + [last]


def ring(axis, up):
    count = lax.axis_size(axis)
    return [(i, (i + 1) % count if up else (i - 1) % count) for i in range(count)]


def body(spectrum):
    length = spectrum.shape[3]
    rows = lax.axis_size("row")
    cols = lax.axis_size("col")
    planes = length // rows
    table = fourier_table(length)
    parts = table_parts(table)
    first_table = np.stack([part.T.reshape(rows, planes, length) for part in parts])
    second_table = jnp.asarray(np.concatenate([parts[p].T for p in TABLE_PARTS], axis=1))
    third_table = jnp.asarray(np.concatenate([parts[p] for p in TABLE_PARTS], axis=0))

    widths = slab_widths(planes)
    slabs = len(widths)
    split = slabs // 2
    start = planes - sum(widths[:split])
    starts = [(start + sum(widths[:slab])) % planes for slab in range(slabs)]

    me = lax.axis_index("row")
    targets = [partner(me, step, rows) for step in range(rows)]
    sources = [sender(me, step, rows) for step in range(rows)]
    pairs = [[(i, partner(i, step, rows)) for i in range(rows)] for step in range(rows)]
    ordered = ordered_blocks(jnp.asarray(first_table), 1, targets)

    order = sorted(range(1, rows), key=lambda s: (-bin(s >> 1).count("1"), -(s & 1), -s))

    members = spectrum.shape[0]
    parts = [(0, range(0, 1)), (0, range(1, members))]
    parts += [(slab, range(0, members)) for slab in range(1, slabs)]

    def first(part, after):
        slab, chosen = parts[part]
        outs = first_transform(
            spectrum, table, ordered, targets, chosen, starts[slab], widths[slab], after
        )
        pieces[part] = [outs[0]] * rows
        for step in order:
            pieces[part][step] = lax.ppermute(outs[step], "row", pairs[step])

    pieces, arrived, levels, edges, halo = {}, {}, {}, {}, {}
    held = None

    def normals(slab, skip=0, count=None):
        nonlocal held
        before_slab, behind_slab = (slab - 1) % slabs, (slab + 1) % slabs
        before = (levels[before_slab], widths[before_slab] - 1) if before_slab in levels else (levels[slab], 0)
        behind = (levels[behind_slab], 0) if behind_slab in levels else (levels[slab], 0)
        if slab == split:
            before = (halo["before"], 0)
        if slab == split - 1:
            behind = (halo["behind"], 0)
        count = widths[slab] - skip if count is None else count
        *held, token = write_normals(
            levels[slab], before, behind, edges[slab], skip, count, starts[slab], planes, held
        )
        return token

    def third(slab, after):
        received = [arrived[part] for part in range(len(parts)) if parts[part][0] == slab]
        levels[slab], edges[slab] = third_transform(
            received, widths[slab], table, third_table, after
        )
        if slab == split:
            halo["before"] = lax.ppermute(levels[split - 1][-1:], "row", ring("row", True))
            halo["behind"] = lax.ppermute(levels[split][:1], "row", ring("row", False))

    def second(part, after):
        from_whom = sources if part else [jnp.int32(step) for step in range(rows)]
        return second_transform(pieces[part], table, second_table, from_whom, cols, after)

    spectral = first_transform(
        spectrum, table, first_table, None, parts[0][1], starts[0], widths[0], ()
    )
    pieces[0] = lax.all_to_all(spectral, "row", split_axis=0, concat_axis=0, tiled=True)
    first(1, (spectral,))
    tokens = {}
    for part in range(len(parts)):
        after = []
        if part >= 2:
            after.append(levels[part - 3] if part >= 3 else arrived[0])
        if part + 1 < len(parts):
            after.append(pieces[part + 1][0])
        elif part >= 4:
            after.append(tokens[part - 4])
            tokens[part - 3] = normals(part - 3, 0, widths[part - 3] - 1)
            after.append(tokens[part - 3])
        spread = second(part, after)
        arrived[part] = lax.all_to_all(spread, "col", split_axis=0, concat_axis=0, tiled=True)
        after = [spread]
        if part + 2 < len(parts):
            first(part + 2, (pieces[part + 1][order[0]],))
            after = [pieces[part + 2][0]]
        if part >= 2:
            slab = part - 2
            if slab - 2 in tokens:
                after.append(tokens[slab - 2])
            third(slab, after)
            if slab >= 2:
                done = widths[slab - 1] - 1 if part + 1 == len(parts) and part >= 4 else 0
                tokens[slab - 1] = normals(slab - 1, done)
            elif slab == 1 and widths[0] > 1:
                tokens[0] = normals(0, 1)
    after = [tokens[key] for key in sorted(tokens)[-1:]]
    if widths[slabs - 2] > 1:
        after = [normals(slabs - 2, 0, widths[slabs - 2] - 1)]
    third(slabs - 1, after)
    normals(slabs - 2, widths[slabs - 2] - 1)
    normals(slabs - 1)
    normals(0, 0, 1)
    return tuple(held)


def solution(mesh):
    return jax.shard_map(
        body,
        mesh=mesh,
        in_specs=(P(None, "row", "col", None),),
        out_specs=(P("row", "col", None), P(None, "row", "col", None)),
        check_vma=False,
    )
```

```python
import functools
import math

import jax
import jax.numpy as jnp
import ml_dtypes
import numpy as np
from jax import lax
from jax.experimental import pallas as pl
from jax.experimental.pallas import tpu as pltpu
from jax.sharding import PartitionSpec as P

EXACT = lax.Precision.HIGHEST
TABLE_PARTS = (0, 1, 2, 0, 1, 0)
VALUE_PARTS = (0, 0, 0, 1, 1, 2)
VMEM_BYTES = 48 * 1024 * 1024
SCALE = 1.0
PATTERN = (6, 6, 10, 16, 22)
LAST = 4


def fourier_table(length):
    wave_number = np.arange(length)[:, None]
    position = np.arange(length)[None, :]
    nyquist = length // 2
    frequency = np.where(wave_number <= nyquist, wave_number, wave_number - nyquist)
    angle = (frequency * position % length) * (2.0 * math.pi / length)
    edge = (wave_number == 0) | (wave_number == nyquist)
    weight = np.where(edge, math.sqrt(1.0 / length), math.sqrt(2.0 / length))
    table = np.where(wave_number <= nyquist, np.cos(angle), np.sin(angle)) * weight
    return table.astype(np.float32)


def table_parts(table):
    parts = []
    rest = table
    for _ in range(3):
        part = rest.astype(ml_dtypes.bfloat16)
        parts.append(part)
        rest = rest - part.astype(np.float32)
    return parts


def value_parts(value):
    high = value.astype(jnp.bfloat16)
    rest = value - high.astype(jnp.float32)
    middle = rest.astype(jnp.bfloat16)
    low = (rest - middle.astype(jnp.float32)).astype(jnp.bfloat16)
    return high, middle, low


def partner(me, step, count):
    if count & (count - 1) == 0:
        return me ^ step
    return (me + step) % count


def sender(me, step, count):
    if count & (count - 1) == 0:
        return me ^ step
    return (me + count - step) % count


ANY = pl.BlockSpec(memory_space=pl.ANY)


def cost(time):
    return pl.CostEstimate(flops=0, bytes_accessed=int(SCALE * time * 3.0e6), transcendentals=0)


def params():
    return pltpu.CompilerParams(vmem_limit_bytes=VMEM_BYTES)


def first_kernel(table_ref, x_ref, *rest, widths, chunk):
    outs = rest[-len(widths) :]
    rows = table_ref.shape[0] // 3
    tile, inner, length = x_ref.shape
    flat = [out.reshape(width * tile, inner) for out, width in zip(outs, widths)]

    @pl.loop(0, tile // chunk)
    def _(part):
        block = x_ref[pl.ds(chunk * part, chunk)].reshape(chunk * inner, length)
        product = lax.dot_general(
            table_ref[...], block, (((1,), (1,)), ((), ())), preferred_element_type=jnp.float32
        )
        total = product[2 * rows :] + product[rows : 2 * rows] + product[:rows]
        at = 0
        for out, width in zip(flat, widths):
            for j in range(chunk):
                out[pl.ds(chunk * part + j, width, stride=tile), :] = total[
                    at : at + width, j * inner : (j + 1) * inner
                ]
            at += width


def ordered_blocks(array, axis, blocks):
    return jnp.concatenate(
        [lax.dynamic_slice_in_dim(array, block, 1, axis=axis) for block in blocks], axis=axis
    )


def first_transform(spectrum, table, ordered, blocks, chosen_members, first, width, after):
    _, span_b, span_q, length = spectrum.shape
    member, members = chosen_members.start, len(chosen_members)
    groups = ordered.shape[1]
    if span_q % 128 or span_b % 8:
        part = spectrum[member : member + members].astype(jnp.float32)
        chosen = jnp.asarray(table).reshape(length, groups, -1)[:, :, first : first + width]
        chosen = chosen if blocks is None else ordered_blocks(chosen, 1, blocks)
        whole = jnp.einsum("cbqk,ksx->scxbq", part, chosen, precision=EXACT)
        return whole if blocks is None else [whole[step] for step in range(groups)]
    operand = jnp.asarray(ordered[:, :, first : first + width].reshape(-1, length))
    tile = 16 if span_b % 16 == 0 else 8
    chunk = 8
    while chunk > 2 and operand.shape[0] * chunk * span_q > 2**18:
        chunk //= 2
    if blocks is None:
        parts = [width * groups]
        out_specs = [
            pl.BlockSpec((groups, None, width, tile, span_q), lambda c, b: (0, c, 0, b, 0))
        ]
        out_shape = [jax.ShapeDtypeStruct((groups, members, width, span_b, span_q), jnp.float32)]
    else:
        parts = [width] * groups
        out_specs = [pl.BlockSpec((None, width, tile, span_q), lambda c, b: (c, 0, b, 0))] * groups
        out_shape = [
            jax.ShapeDtypeStruct((members, width, span_b, span_q), jnp.float32)
        ] * groups
    outs = pl.pallas_call(
        functools.partial(first_kernel, widths=parts, chunk=chunk),
        grid=(members, span_b // tile),
        in_specs=[
            pl.BlockSpec(operand.shape, lambda c, b: (0, 0)),
            pl.BlockSpec((None, tile, span_q, length), lambda c, b: (member + c, b, 0, 0)),
        ]
        + [ANY] * len(after),
        out_specs=out_specs,
        out_shape=out_shape,
        compiler_params=params(),
        cost_estimate=cost(12 + width),
        name="first",
    )(operand, spectrum, *after)
    return outs[0] if blocks is None else outs


def edge_rows(width):
    rows = 8
    while rows < 2 * width:
        rows *= 2
    return rows


def second_kernel(sources_ref, table_ref, *rest, count, planes, span_y):
    ins, out_ref, value_ref = rest[:count], rest[-2], rest[-1]
    tile, span_b, span_q = ins[0].shape
    groups = out_ref.shape[0]
    length = groups * span_y
    first = pl.program_id(1) * tile
    for step in range(count):
        at = pl.multiple_of(sources_ref[step] * span_b, 8)
        for j in range(tile):
            value_ref[pl.ds(at, span_b), j * span_q : (j + 1) * span_q] = ins[step][j]
    parts = value_parts(value_ref[...])
    stacked = jnp.concatenate([parts[p] for p in VALUE_PARTS], axis=0)
    product = jnp.dot(table_ref[...], stacked, preferred_element_type=jnp.float32)

    @pl.when(first == 0)
    def _():
        rest_rows = out_ref.shape[1] - planes * span_y
        out_ref[:, planes * span_y :, :] = jnp.zeros((groups, rest_rows, span_q), jnp.float32)

    for j in range(tile):
        field = product[:, j * span_q : (j + 1) * span_q]
        at = pl.multiple_of((first + j) * span_y, 8)
        out_ref[:, pl.ds(at, span_y), :] = field.reshape(groups, span_y, span_q)
        edge = planes * span_y + 2 * (first + j)
        for g in range(groups):
            before = (g * span_y - 1) % length
            behind = (g + 1) * span_y % length
            out_ref[g, pl.ds(edge, 1), :] = field[before : before + 1]
            out_ref[g, pl.ds(edge + 1, 1), :] = field[behind : behind + 1]


def second_transform(pieces, table, stacked, sources, groups, after):
    count = len(pieces)
    members, width, span_b, span_q = pieces[0].shape
    length = count * span_b
    span_y = length // groups
    edge = edge_rows(width)
    out_shape = (groups, members, width * span_y + edge, span_q)
    if span_q % 128 or span_b % 8 or span_y % 8:
        chosen = ordered_blocks(jnp.asarray(table).reshape(count, span_b, length), 0, sources)
        pieces = jnp.stack([pieces[step] for step in range(count)])
        field = jnp.einsum("scabq,sby->cayq", pieces, chosen, precision=EXACT)
        inner = field.reshape(members, width, groups, span_y, span_q)
        inner = inner.transpose(2, 0, 1, 3, 4).reshape(groups, members, width * span_y, span_q)
        before = jnp.roll(field, 1, axis=2)[:, :, ::span_y]
        behind = jnp.roll(field, -1, axis=2)[:, :, span_y - 1 :: span_y]
        edges = jnp.stack([before, behind], axis=2).transpose(3, 0, 1, 2, 4)
        edges = edges.reshape(groups, members, 2 * width, span_q)
        edges = jnp.pad(edges, ((0, 0), (0, 0), (0, edge - 2 * width), (0, 0)))
        return jnp.concatenate([inner, edges], axis=2)
    tile = 2 if width % 2 == 0 else 1
    if isinstance(pieces, list):
        in_specs = [pl.BlockSpec((None, tile, span_b, span_q), lambda c, a: (c, a, 0, 0))] * count
    else:
        in_specs = [
            pl.BlockSpec((None, None, tile, span_b, span_q), lambda c, a, s=s: (s, c, a, 0, 0))
            for s in range(count)
        ]
        pieces = [pieces] * count
    return pl.pallas_call(
        functools.partial(second_kernel, count=count, planes=width, span_y=span_y),
        grid=(members, width // tile),
        in_specs=[
            pl.BlockSpec(memory_space=pltpu.SMEM),
            pl.BlockSpec(stacked.shape, lambda c, a: (0, 0)),
        ]
        + in_specs
        + [ANY] * len(after),
        out_specs=pl.BlockSpec((groups, None, out_shape[2], span_q), lambda c, a: (0, c, 0, 0)),
        out_shape=jax.ShapeDtypeStruct(out_shape, jnp.float32),
        scratch_shapes=[pltpu.VMEM((length, tile * span_q), jnp.float32)],
        compiler_params=params(),
        cost_estimate=cost(1 + 2 * width),
        name="second",
    )(jnp.stack(sources).astype(jnp.int32), stacked, *pieces, *after)


def third_kernel(table_ref, *rest, firsts, together):
    out_ref, edge_ref = rest[-2:]
    ins, edge_ins = rest[: len(firsts)], rest[len(firsts) : 2 * len(firsts)]
    member = pl.program_id(1)

    def value_of(refs):
        value = None
        for ref, first in zip(refs, firsts):
            here = jnp.concatenate([ref[g] for g in range(ref.shape[0])], axis=1)
            value = here if value is None else jnp.where(member >= first, here, value)
        return value

    def level_of(value):
        parts = value_parts(value)
        stacked = jnp.concatenate([parts[p] for p in VALUE_PARTS], axis=1)
        field = jnp.dot(stacked, table_ref[...], preferred_element_type=jnp.float32)
        return 0.5 * (field * field)

    def add(ref, level):
        @pl.when(member == 0)
        def _():
            ref[...] = level

        @pl.when(member > 0)
        def _():
            ref[...] += level

    if together:
        level = level_of(jnp.concatenate([value_of(ins), value_of(edge_ins)], axis=0))
        rows = level.shape[0] - edge_ref.shape[0]
        add(out_ref, level[:rows].reshape(out_ref.shape))
        add(edge_ref, level[rows:])
        return
    add(out_ref, level_of(value_of(ins)).reshape(out_ref.shape))

    @pl.when(pl.program_id(0) == 0)
    def _():
        add(edge_ref, level_of(value_of(edge_ins)))


def third_transform(received, width, table, stacked, after):
    groups, _, rows, span_q = received[0].shape
    edge = edge_rows(width)
    span_y = (rows - edge) // width
    length = groups * span_q
    if span_q % 128 or span_y % 8:
        chosen = jnp.asarray(table).reshape(groups, span_q, length)
        received = jnp.concatenate(received, axis=1)
        field = jnp.einsum("scrq,sqz->crz", received, chosen, precision=EXACT)
        level = 0.5 * jnp.sum(field * field, axis=0)
        return level[: width * span_y].reshape(width, span_y, length), level[width * span_y :]
    tile = 4 if width == 4 else 2 if width % 2 == 0 else 1
    counts = [array.shape[1] for array in received]
    firsts = [sum(counts[:k]) for k in range(len(counts))]

    def spec(block_rows, block_of, first, count):
        return pl.BlockSpec(
            (groups, None, block_rows, span_q),
            lambda a, c: (0, jnp.clip(c - first, 0, count - 1), block_of(a), 0),
        )

    return pl.pallas_call(
        functools.partial(third_kernel, firsts=firsts, together=width == tile),
        grid=(width // tile, sum(counts)),
        in_specs=[pl.BlockSpec(stacked.shape, lambda a, c: (0, 0))]
        + [spec(tile * span_y, lambda a: a, *one) for one in zip(firsts, counts)]
        + [spec(edge, lambda a: width * span_y // edge, *one) for one in zip(firsts, counts)]
        + [ANY] * len(after),
        out_specs=[
            pl.BlockSpec((tile, span_y, length), lambda a, c: (a, 0, 0)),
            pl.BlockSpec((edge, length), lambda a, c: (0, 0)),
        ],
        out_shape=[
            jax.ShapeDtypeStruct((width, span_y, length), jnp.float32),
            jax.ShapeDtypeStruct((edge, length), jnp.float32),
        ],
        compiler_params=params(),
        cost_estimate=cost(1 + 2 * width),
        name="third",
    )(stacked, *received, *received, *after)


def normal_kernel(centre_ref, before_ref, behind_ref, edge_ref, *rest, skip, base):
    level_ref, normal_ref, token_ref = rest[-3:]
    width, span_y, length = centre_ref.shape
    i = pl.program_id(0) + skip
    centre = centre_ref[i]
    before = jnp.where(i == 0, before_ref[0], centre_ref[jnp.maximum(i - 1, 0)])
    behind = jnp.where(i == width - 1, behind_ref[0], centre_ref[jnp.minimum(i + 1, width - 1)])
    row = lax.broadcasted_iota(jnp.int32, (span_y, length), 0)
    left = jnp.where(row == 0, edge_ref[pl.ds(2 * (base + i), 1), :], pltpu.roll(centre, 1, 0))
    right = jnp.where(
        row == span_y - 1, edge_ref[pl.ds(2 * (base + i) + 1, 1), :], pltpu.roll(centre, span_y - 1, 0)
    )
    step_x = 0.5 * (behind - before)
    step_y = 0.5 * (right - left)
    step_z = 0.5 * (pltpu.roll(centre, length - 1, 1) - pltpu.roll(centre, 1, 1))
    magnitude = jnp.sqrt(step_x * step_x + step_y * step_y + step_z * step_z)
    inverse = -1.0 / jnp.maximum(magnitude, 1.0)
    level_ref[0] = centre
    token_ref[...] = jnp.zeros_like(token_ref)
    normal_ref[0, 0] = (step_x * inverse).astype(jnp.bfloat16)
    normal_ref[1, 0] = (step_y * inverse).astype(jnp.bfloat16)
    normal_ref[2, 0] = (step_z * inverse).astype(jnp.bfloat16)


def write_normals(centre, before, behind, edge, skip, count, first, whole, held):
    width, span_y, length = centre.shape
    span, base = width, 0
    if count == 1:
        span, base = 1, skip
        before = (centre, skip - 1) if skip else before
        behind = (centre, skip + 1) if skip < width - 1 else behind
    before, before_at = before
    behind, behind_at = behind
    held = () if held is None else held
    return pl.pallas_call(
        functools.partial(normal_kernel, skip=skip - base, base=base),
        grid=(count,),
        in_specs=[
            pl.BlockSpec((span, span_y, length), lambda i: (base, 0, 0)),
            pl.BlockSpec((1, span_y, length), lambda i: (before_at, 0, 0)),
            pl.BlockSpec((1, span_y, length), lambda i: (behind_at, 0, 0)),
            pl.BlockSpec(edge.shape, lambda i: (0, 0)),
        ]
        + [ANY] * len(held),
        out_specs=[
            pl.BlockSpec((1, span_y, length), lambda i: (first + skip + i, 0, 0)),
            pl.BlockSpec((3, 1, span_y, length), lambda i: (0, first + skip + i, 0, 0)),
            pl.BlockSpec((8, 128), lambda i: (0, 0)),
        ],
        out_shape=[
            jax.ShapeDtypeStruct((whole, span_y, length), jnp.float32),
            jax.ShapeDtypeStruct((3, whole, span_y, length), jnp.bfloat16),
            jax.ShapeDtypeStruct((8, 128), jnp.float32),
        ],
        input_output_aliases={4 + k: k for k in range(len(held))},
        compiler_params=params(),
        cost_estimate=cost(1 + count / 2),
        name="normals",
    )(centre, before, behind, edge, *held)


def slab_widths(planes):
    last = min(LAST, max(planes // 4, 1))
    left = planes - last
    widths = []
    while left:
        width = min(PATTERN[min(len(widths), len(PATTERN) - 1)], left)
        widths.append(width)
        left -= width
    return widths + [last]


def ring(axis, up):
    count = lax.axis_size(axis)
    return [(i, (i + 1) % count if up else (i - 1) % count) for i in range(count)]


def body(spectrum):
    length = spectrum.shape[3]
    rows = lax.axis_size("row")
    cols = lax.axis_size("col")
    planes = length // rows
    table = fourier_table(length)
    parts = table_parts(table)
    first_table = np.stack([part.T.reshape(rows, planes, length) for part in parts])
    second_table = jnp.asarray(np.concatenate([parts[p].T for p in TABLE_PARTS], axis=1))
    third_table = jnp.asarray(np.concatenate([parts[p] for p in TABLE_PARTS], axis=0))

    widths = slab_widths(planes)
    slabs = len(widths)
    split = slabs // 2
    start = planes - sum(widths[:split])
    starts = [(start + sum(widths[:slab])) % planes for slab in range(slabs)]

    me = lax.axis_index("row")
    targets = [partner(me, step, rows) for step in range(rows)]
    sources = [sender(me, step, rows) for step in range(rows)]
    pairs = [[(i, partner(i, step, rows)) for i in range(rows)] for step in range(rows)]
    ordered = ordered_blocks(jnp.asarray(first_table), 1, targets)

    order = sorted(range(1, rows), key=lambda s: (-bin(s >> 1).count("1"), -(s & 1), -s))

    members = spectrum.shape[0]
    parts = [(0, range(0, 1)), (0, range(1, members))]
    parts += [(slab, range(0, members)) for slab in range(1, slabs)]

    def first(part, after):
        slab, chosen = parts[part]
        outs = first_transform(
            spectrum, table, ordered, targets, chosen, starts[slab], widths[slab], after
        )
        pieces[part] = [outs[0]] * rows
        for step in order:
            pieces[part][step] = lax.ppermute(outs[step], "row", pairs[step])

    pieces, arrived, levels, edges, halo = {}, {}, {}, {}, {}
    held = None

    def normals(slab, skip=0, count=None):
        nonlocal held
        before_slab, behind_slab = (slab - 1) % slabs, (slab + 1) % slabs
        before = (levels[before_slab], widths[before_slab] - 1) if before_slab in levels else (levels[slab], 0)
        behind = (levels[behind_slab], 0) if behind_slab in levels else (levels[slab], 0)
        if slab == split:
            before = (halo["before"], 0)
        if slab == split - 1:
            behind = (halo["behind"], 0)
        count = widths[slab] - skip if count is None else count
        *held, token = write_normals(
            levels[slab], before, behind, edges[slab], skip, count, starts[slab], planes, held
        )
        return token

    def third(slab, after):
        received = [arrived[part] for part in range(len(parts)) if parts[part][0] == slab]
        levels[slab], edges[slab] = third_transform(
            received, widths[slab], table, third_table, after
        )
        if slab == split:
            halo["before"] = lax.ppermute(levels[split - 1][-1:], "row", ring("row", True))
            halo["behind"] = lax.ppermute(levels[split][:1], "row", ring("row", False))

    def second(part, after):
        from_whom = sources if part else [jnp.int32(step) for step in range(rows)]
        return second_transform(pieces[part], table, second_table, from_whom, cols, after)

    spectral = first_transform(
        spectrum, table, first_table, None, parts[0][1], starts[0], widths[0], ()
    )
    pieces[0] = lax.all_to_all(spectral, "row", split_axis=0, concat_axis=0, tiled=True)
    first(1, (spectral,))
    tokens = {}
    for part in range(len(parts)):
        after = []
        if part >= 2:
            after.append(levels[part - 3] if part >= 3 else arrived[0])
        if part + 1 < len(parts):
            after.append(pieces[part + 1][0])
        elif part >= 4:
            after.append(tokens[part - 4])
            tokens[part - 3] = normals(part - 3, 0, widths[part - 3] - 1)
            after.append(tokens[part - 3])
        spread = second(part, after)
        arrived[part] = lax.all_to_all(spread, "col", split_axis=0, concat_axis=0, tiled=True)
        after = [spread]
        if part + 2 < len(parts):
            first(part + 2, (pieces[part + 1][order[0]],))
            after = [pieces[part + 2][0]]
        if part >= 2:
            slab = part - 2
            if slab - 2 in tokens:
                after.append(tokens[slab - 2])
            third(slab, after)
            if slab >= 2:
                done = widths[slab - 1] - 1 if part + 1 == len(parts) and part >= 4 else 0
                tokens[slab - 1] = normals(slab - 1, done)
            elif slab == 1 and widths[0] > 1:
                tokens[0] = normals(0, 1)
    after = [tokens[key] for key in sorted(tokens)[-1:]]
    if widths[slabs - 2] > 1:
        after = [normals(slabs - 2, 0, widths[slabs - 2] - 1)]
    third(slabs - 1, after)
    normals(slabs - 2, widths[slabs - 2] - 1)
    normals(slabs - 1)
    normals(0, 0, 1)
    return tuple(held)


def solution(mesh):
    return jax.shard_map(
        body,
        mesh=mesh,
        in_specs=(P(None, "row", "col", None),),
        out_specs=(P("row", "col", None), P(None, "row", "col", None)),
        check_vma=False,
    )
```
